768 devices in a mesh: seq: 96 (over x, y, z_lo), head: 8 (over z_hi, core).
Axes of the slice: x: 4, y: 8, z: 12 (z_hi: 4, z_lo: 3; z = z_hi * 3 + z_lo), core: 2. Of those that a mesh axis runs over, the one named last changes fastest.
Arguments:
- query_heads: bfloat16 [12288, 3072], P('seq', 'head'), may hold values from -6 to 6
- key_heads: bfloat16 [12288, 1024], P('seq', 'head'), may hold values from -6 to 6
- value_heads: bfloat16 [12288, 1024], P('seq', 'head'), may hold values from -6 to 6
- out_weight: bfloat16 [3072, 3072], P('head'), may hold values from -0.109375 to 0.109375
- out_grad: bfloat16 [12288, 3072], P('seq', 'head'), may hold values from -6 to 6
- clip_lengths: int32 [8], replicated, may hold values from 1 to 3072, 12288 in all
Outputs:
- mixed: bfloat16 [12288, 3072], P('seq', 'head')
- attended: bfloat16 [12288, 3072], P('seq', 'head')
- d_queries: bfloat16 [12288, 3072], P('seq', 'head')
- d_keys: bfloat16 [12288, 1024], P('seq', 'head')
- d_values: bfloat16 [12288, 1024], P('seq', 'head')
The draws below stay inside these ranges and needn't reach their ends.
Inputs may be any that keep to these rules, and one draw needn't show every extreme that they name: `clip_lengths`: the longest clip has exactly 3072 tokens and all sum to 12288.
All inputs are finite; a program needn't handle non-finite values.
Results may differ from the reference program's by a relative error of at most 0.03.
Values may be sent and summed in bfloat16 or wider, within the bound.
A program may use at most 32 MiB of HBM per device.

```python
import math
import jax
import jax.numpy as jnp
import numpy as np
from jax import lax

D = 3072
HEADS = 24
KV_HEADS = 8
HD = 128
TOK_DEV = 128
SPAN = 24
CLIPS = 8
TOKENS = 12288
CLIP_MOST = 3072
N_HEAD = 8


def draw_query_heads(key, part):
    base_key = jax.random.fold_in(key, 1)
    result = jnp.clip(jax.random.normal(base_key, (TOKENS, HEADS, HD), jnp.float32), -4.0, 4.0)
    return result.reshape(TOKENS, HEADS * HD).astype(jnp.bfloat16)


def draw_key_heads(key, part):
    base_key = jax.random.fold_in(key, 2)
    result = jnp.clip(jax.random.normal(base_key, (TOKENS, KV_HEADS, HD), jnp.float32), -4.0, 4.0)
    return result.reshape(TOKENS, KV_HEADS * HD).astype(jnp.bfloat16)


def block_scale(stream_key, extent, split, smallest, high):
    def one(axis_at, parts):
        heights = jax.random.uniform(jax.random.fold_in(jax.random.fold_in(stream_key, 6), axis_at), (parts,), jnp.float32, smallest / len(split), high / len(split))
        return jnp.repeat(jnp.exp(heights), extent[axis_at] // parts).reshape((-1,) + (1,) * (len(extent) - axis_at - 1))

    level = one(*split[0])
    for cut in split[1:]:
        level = level * one(*cut)
    return level


def length_profile(amount, total, limit, lean):
    loads = [(1 << 20) // math.isqrt(rank ** lean) + 1 for rank in range(2, amount + 1)]
    spare, given = total - limit - (amount - 1), [1] * (amount - 1)
    while spare > 0:
        candidates = [i for i in range(amount - 1) if given[i] < limit]
        mass, left = sum([loads[i] for i in candidates]), spare
        for i in candidates:
            extra = min(limit - given[i], max(1, left * loads[i] // mass), spare)
            given[i] = given[i] + extra
            spare = spare - extra
    return np.array([limit] + given)


def ragged_sizes(stream_key, number_of, total, reach, slope):
    if number_of == 2:
        one = jax.random.randint(stream_key, (), max(1, total - reach), min(reach, total - 1) + 1)
        return jnp.stack([one, total - one])
    lengths = jnp.asarray(length_profile(number_of, total, reach, slope), jnp.int32)
    pairs = (number_of - 1) // 2
    donor, sink = lengths[1:1 + 2 * pairs:2], lengths[2:2 + 2 * pairs:2]
    room = jnp.minimum(donor - 1, reach - sink)
    shifted = jax.random.randint(jax.random.fold_in(stream_key, 1), (pairs,), 0, 1 << 20) % (room + 1)
    lengths = lengths.at[1:1 + 2 * pairs:2].set(donor - shifted).at[2:2 + 2 * pairs:2].set(sink + shifted)
    return lengths[jax.random.permutation(jax.random.fold_in(stream_key, 2), number_of)]


def centred(own_key, shape, spread, limit, pieces=(), held_as=jnp.bfloat16):
    values = jax.random.normal(own_key, shape, jnp.float32) * spread
    if len(pieces) > 0:
        values = block_scale(own_key, shape, pieces, -0.22, 0.18) * values
    return jnp.clip(values, min=-limit, max=limit).astype(held_as)


def setup_inputs(seed: int = 0) -> dict:
    splits = jax.random.split(jax.random.key(seed), 7)
    query_heads = draw_query_heads(jax.random.fold_in(splits[6], 71), 0)
    key_heads = draw_key_heads(jax.random.fold_in(splits[6], 71), 0)
    value_heads = centred(splits[2], (TOKENS, KV_HEADS * HD), 1.0, 6.0, ((0, 96), (1, 8)))
    out_weight = centred(splits[3], (HEADS * HD, D), (HEADS * HD) ** -0.5, 0.109375, ((0, 8),))
    out_grad = centred(splits[4], (TOKENS, D), 1.0, 6.0, ((0, 96), (1, 8)))
    clip_lengths = ragged_sizes(splits[5], CLIPS, TOKENS, CLIP_MOST, 2).astype(jnp.int32)
    return dict(query_heads=query_heads, key_heads=key_heads, value_heads=value_heads, out_weight=out_weight, out_grad=out_grad, clip_lengths=clip_lengths)


def clip_index(positions, clip_lengths):
    clip_ends = jnp.cumsum(clip_lengths).astype(jnp.int32)
    return lax.optimization_barrier(jnp.sum((positions[:, None] >= clip_ends[None, :]).astype(jnp.int32), axis=1)).astype(jnp.int32)

def reference(query_heads, key_heads, value_heads, out_weight, out_grad, clip_lengths):
    group_size = HEADS // KV_HEADS
    lead_rows = SPAN * TOK_DEV
    key_width = lead_rows + TOK_DEV
    score_scale = 1.0 / math.sqrt(HD)
    blocks = TOKENS // TOK_DEV
    d_heads = jnp.dot(out_grad, out_weight.T, preferred_element_type=jnp.float32).astype(jnp.bfloat16)
    zero_rows = jnp.zeros((lead_rows, KV_HEADS * HD), key_heads.dtype)
    key_pad = jnp.concatenate([zero_rows, key_heads], 0)
    value_pad = jnp.concatenate([zero_rows, value_heads], 0)
    pad_pos = (jnp.arange(TOKENS + lead_rows, dtype=jnp.int32) - lead_rows).astype(jnp.int32)
    pad_clip = jnp.where(pad_pos >= 0, clip_index(pad_pos, clip_lengths), -1).astype(jnp.int32)

    def one_block(running, block_num):
        dk_pad, dv_pad = running
        first_row = (block_num * TOK_DEV).astype(jnp.int32)
        query_grid = lax.dynamic_slice_in_dim(query_heads, first_row, TOK_DEV, 0).reshape(TOK_DEV, KV_HEADS, group_size, HD).astype(jnp.float32)
        grad_grid = lax.dynamic_slice_in_dim(d_heads, first_row, TOK_DEV, 0).reshape(TOK_DEV, KV_HEADS, group_size, HD).astype(jnp.float32)
        key_win = lax.dynamic_slice_in_dim(key_pad, first_row, key_width, 0).reshape(key_width, KV_HEADS, HD).astype(jnp.float32)
        value_win = lax.dynamic_slice_in_dim(value_pad, first_row, key_width, 0).reshape(key_width, KV_HEADS, HD).astype(jnp.float32)
        key_pos = lax.dynamic_slice_in_dim(pad_pos, first_row, key_width, 0)
        key_clip = lax.dynamic_slice_in_dim(pad_clip, first_row, key_width, 0)
        query_pos = (first_row + jnp.arange(TOK_DEV, dtype=jnp.int32)).astype(jnp.int32)
        query_clip = clip_index(query_pos, clip_lengths)
        allowed = (query_clip[:, None] == key_clip[None, :]) & (key_pos[None, :] <= query_pos[:, None])
        scores = jnp.einsum('tgcd,sgd->gcts', query_grid, key_win) * score_scale
        scores = jnp.where(allowed, scores, -1e+30)
        row_max = lax.optimization_barrier(jnp.max(scores, axis=-1, keepdims=True))
        row_total = lax.optimization_barrier(jnp.sum(jnp.exp(scores - row_max), axis=-1, keepdims=True))
        probabilities = jnp.exp(scores - (row_max + jnp.log(row_total)))
        weights = probabilities.astype(jnp.bfloat16)
        attended_grid = jnp.einsum('gcts,sgd->tgcd', weights.astype(jnp.float32), value_win).astype(jnp.bfloat16)
        row_delta = lax.optimization_barrier(jnp.sum(grad_grid * attended_grid.astype(jnp.float32), axis=-1))
        row_delta = jnp.transpose(row_delta, (1, 2, 0))[..., None]
        dprob = jnp.einsum('tgcd,sgd->gcts', grad_grid, value_win)
        dscores = (probabilities * (dprob - row_delta)).astype(jnp.bfloat16)
        dscore_wide = dscores.astype(jnp.float32)
        dquery = (jnp.einsum('gcts,sgd->tgcd', dscore_wide, key_win) * score_scale).astype(jnp.bfloat16)
        dkey_part = (jnp.einsum('gcts,tgcd->sgd', dscore_wide, query_grid) * score_scale).reshape(key_width, KV_HEADS * HD)
        dvalue_part = jnp.einsum('gcts,tgcd->sgd', weights.astype(jnp.float32), grad_grid).reshape(key_width, KV_HEADS * HD)
        dk_pad = lax.dynamic_update_slice_in_dim(dk_pad, lax.dynamic_slice_in_dim(dk_pad, first_row, key_width, 0) + dkey_part, first_row, 0)
        dv_pad = lax.dynamic_update_slice_in_dim(dv_pad, lax.dynamic_slice_in_dim(dv_pad, first_row, key_width, 0) + dvalue_part, first_row, 0)
        return ((dk_pad, dv_pad), (attended_grid.reshape(TOK_DEV, HEADS * HD), dquery.reshape(TOK_DEV, HEADS * HD)))
    empty = jnp.zeros((TOKENS + lead_rows, KV_HEADS * HD), jnp.float32)
    (dk_pad, dv_pad), (attended_parts, dquery_parts) = lax.scan(one_block, (empty, empty), jnp.arange(blocks, dtype=jnp.int32))
    attended = attended_parts.reshape(TOKENS, HEADS * HD)
    d_queries = dquery_parts.reshape(TOKENS, HEADS * HD)
    group_cols = HEADS * HD // N_HEAD

    def add_group(total, group_num):
        first_col = (group_num * group_cols).astype(jnp.int32)
        cols = lax.dynamic_slice_in_dim(attended, first_col, group_cols, 1)
        rows = lax.dynamic_slice_in_dim(out_weight, first_col, group_cols, 0)
        part = jnp.dot(cols, rows, preferred_element_type=jnp.float32).astype(jnp.bfloat16)
        return (total + part.astype(jnp.float32), None)
    mixed_sum, _ = lax.scan(add_group, jnp.zeros((TOKENS, D), jnp.float32), jnp.arange(N_HEAD, dtype=jnp.int32))
    mixed = mixed_sum.astype(jnp.bfloat16)
    return (mixed, attended, d_queries, dk_pad[lead_rows:].astype(jnp.bfloat16), dv_pad[lead_rows:].astype(jnp.bfloat16))
```

```python
import math

import jax
import jax.numpy as jnp
from jax import lax
from jax.experimental import pallas as pl
from jax.experimental.pallas import tpu as pltpu
from jax.sharding import PartitionSpec as P

HD = 128
GROUP = 3
TOK = 128
LO = 3
LINKS = 32
REACH = 8
N_SEQ = LO * LINKS
N_HEAD = 8
N_HI = 4
WIDTH = GROUP * HD
BUNDLE = LO * TOK
SCALE = 1.0 / math.sqrt(HD)
EXP2_SCALE = SCALE * math.log2(math.e)
MASKED = -1e30
MESH = pl.DeviceIdType.MESH
F32 = jnp.float32
BF16 = jnp.bfloat16


def mm(a, b):
    return jnp.dot(a, b, preferred_element_type=F32)


def mm_t(a, b):
    return lax.dot_general(a, b, (((1,), (1,)), ((), ())), preferred_element_type=F32)


def blocks_t(x):
    if x.shape[0] == HD:
        return jnp.concatenate([x[:, i * HD:(i + 1) * HD].T for i in range(GROUP)], axis=0)
    return jnp.concatenate([x[i * HD:(i + 1) * HD, :].T for i in range(GROUP)], axis=1)


def kernel(
    clip_ref, q_ref, k_ref, v_ref, og_ref, w_hbm,
    mixed_ref, att_ref, dq_ref, dk_ref, dv_ref,
    kv, og, w, qt, qs, dot, dos, start, s_buf, p_buf, kt, vt, mx, acc,
    part, psib, pmine, pfar, up_in, down_in, stage, zs, zr,
    w_sem, kv_send, kv_recv, og_send, og_recv, osib_send, osib_recv,
    part_send, part_recv, pfar_send, pfar_recv,
    up_send, up_recv, down_send, down_recv, z_send, z_recv,
):
    s = lax.axis_index("seq")
    n = lax.axis_index("head")
    link, z = lax.div(s, LO), lax.rem(s, LO)
    hi, core = lax.div(n, 2), lax.rem(n, 2)

    def at_link(step):
        return (lax.rem(s + step * LO + N_SEQ, N_SEQ), n)

    def at_lo(r):
        return (link * LO + lax.rem(z + r, LO), n)

    def at_hi(d):
        return (s, lax.rem(hi + d, N_HI) * 2 + core)

    sibling = (s, hi * 2 + 1 - core)
    lo_of = [lax.rem(z + LO - r, LO) for r in range(LO)]

    def copy(src, dst, ssem, rsem, dev):
        return pltpu.make_async_remote_copy(
            src_ref=src, dst_ref=dst, send_sem=ssem, recv_sem=rsem, device_id=dev, device_id_type=MESH
        )

    sent = []

    def go(c):
        c.start()
        sent.append(c)

    w_copy = pltpu.make_async_copy(w_hbm, w, w_sem)
    w_copy.start()
    kv[0, z, 0] = k_ref[...]
    kv[0, z, 1] = v_ref[...]
    og[n] = og_ref[...]

    barrier = pltpu.get_barrier_semaphore()
    partners = [at_link(1), at_link(-1), at_link(REACH), at_link(-REACH), at_lo(1), at_lo(2)]
    partners += [sibling] + [at_hi(d) for d in (1, 2, 3)]
    for dev in partners:
        pl.semaphore_signal(barrier, inc=1, device_id=dev, device_id_type=MESH)
    pl.semaphore_wait(barrier, len(partners))

    def z_copy(r):
        return copy(kv.at[0, z], kv.at[0, z], kv_send.at[0, r], kv_recv.at[0, r], at_lo(r))

    def up_copy(k, r):
        return copy(kv.at[k - 1, lo_of[r]], kv.at[k, lo_of[r]], kv_send.at[k, r], kv_recv.at[k, r], at_link(1))

    def down_copy(k, r):
        if k == REACH:
            return copy(kv.at[0, lo_of[r]], kv.at[k, lo_of[r]], kv_send.at[k, r], kv_recv.at[k, r], at_link(REACH))
        return copy(kv.at[k + 1, lo_of[r]], kv.at[k, lo_of[r]], kv_send.at[k, r], kv_recv.at[k, r], at_link(-1))

    def og_copy(d):
        return copy(og.at[n], og.at[n], og_send.at[d], og_recv.at[d], at_hi(d))

    def sib_copy(d):
        m = lax.rem(hi + N_HI - d, N_HI) * 2 + core
        return copy(og.at[m], og.at[m], osib_send.at[d], osib_recv.at[d], sibling)

    go(up_copy(1, 0))
    go(down_copy(REACH, 0))
    for r in (1, 2):
        go(z_copy(r))
    for d in (2, 1, 3):
        go(og_copy(d))
    go(sib_copy(0))

    q_t = jnp.concatenate([q_ref[:, i * HD:(i + 1) * HD].astype(F32).T for i in range(GROUP)], axis=1)
    qt[...] = q_t.astype(BF16)
    lane = lax.broadcasted_iota(jnp.int32, (1, WIDTH), 1)
    pos = s * TOK + lax.rem(lane, TOK)
    begin = jnp.zeros_like(pos)
    end = jnp.int32(0)
    for i in range(8):
        end = end + clip_ref[i]
        begin = jnp.where(pos >= end, end, begin)
    start[...] = jnp.broadcast_to(begin, start.shape)

    for r in (1, 2):
        z_copy(r).wait_recv()
        go(up_copy(1, r))
        go(down_copy(REACH, r))

    def scores(k, first=False):
        keys = kv[k, :, 0].reshape(BUNDLE, HD)
        sc = mm(keys, qt[...])
        row = (link - k) * BUNDLE + lax.broadcasted_iota(jnp.int32, (BUNDLE, WIDTH), 0)
        ok = row >= start[0:1, :]
        if k == 0:
            ok = ok & (row <= pos)
        sc = jnp.where(ok, sc, MASKED)
        s_buf[k] = sc
        top = jnp.max(sc.reshape(BUNDLE // 8, 8, WIDTH), axis=0)
        mx[...] = top if first else jnp.maximum(mx[...], top)
        for i in range(LO):
            cols = slice(k * BUNDLE + i * TOK, k * BUNDLE + (i + 1) * TOK)
            kt[:, cols] = kv[k, i, 0].T
            vt[:, cols] = kv[k, i, 1].T

    scores(0, True)
    for step in range(1, 5):
        up, down = step, REACH + 1 - step
        for r in range(LO):
            up_copy(up, r).wait_recv()
            if step < 4:
                go(up_copy(up + 1, r))
            down_copy(down, r).wait_recv()
            if step < 4:
                go(down_copy(down - 1, r))
        if step == 2:
            for d in (1, 3):
                og_copy(d).wait_recv()
                go(sib_copy(d))
        if step == 3:
            og_copy(2).wait_recv()
            go(sib_copy(2))
        scores(up)
        scores(down)

    w_copy.wait()
    for d in range(N_HI):
        sib_copy(d).wait_recv()
    dh = mm_t(w[:, 0:WIDTH], og[0])
    for m in range(1, N_HEAD):
        dh = dh + mm_t(w[:, m * WIDTH:(m + 1) * WIDTH], og[m])
    dh_t = jnp.concatenate([dh[i * HD:(i + 1) * HD, :] for i in range(GROUP)], axis=1)
    dot[...] = dh_t.astype(BF16)

    top = jnp.max(mx[...], axis=0, keepdims=True) * EXP2_SCALE
    total = jnp.zeros((8, WIDTH), F32)
    for k in range(REACH + 1):
        p = jnp.exp2(s_buf[k] * EXP2_SCALE - top)
        total = total + jnp.sum(p.reshape(BUNDLE // 8, 8, WIDTH), axis=0)
        p_buf[k * BUNDLE:(k + 1) * BUNDLE, :] = p.astype(BF16)
    inv = 1.0 / jnp.sum(total, axis=0, keepdims=True)
    out_t = (mm(vt[...], p_buf[...]) * inv).astype(BF16).astype(F32)
    attended = jnp.concatenate([out_t[:, i * HD:(i + 1) * HD].T for i in range(GROUP)], axis=1).astype(BF16)
    att_ref[...] = attended
    d_t = dot[...].astype(F32)
    delta = jnp.sum(d_t * out_t, axis=0, keepdims=True)
    dos[...] = blocks_t(d_t * inv).astype(BF16)
    qs[...] = blocks_t(qt[...].astype(F32) * (inv * SCALE)).astype(BF16)

    def backward(k):
        rows = slice(k * BUNDLE, (k + 1) * BUNDLE)
        p = p_buf[rows, :]
        dp = mm(kv[k, :, 1].reshape(BUNDLE, HD), dot[...])
        ds = (p.astype(F32) * (dp - delta)).astype(BF16)
        acc[1] = mm(p, dos[...]).reshape(LO, TOK, HD)
        acc[0] = mm(ds, qs[...]).reshape(LO, TOK, HD)
        p_buf[rows, :] = ds

    def up_back(k, i):
        return copy(stage.at[k, i], up_in.at[k - 1, i], up_send.at[k - 1, i], up_recv.at[k - 1, i], at_link(-1))

    def down_back(k, i):
        dev = at_link(-REACH) if k == REACH else at_link(1)
        return copy(stage.at[k, i], down_in.at[k - 5, i], down_send.at[k - 5, i], down_recv.at[k - 5, i], dev)

    def send_up(k):
        backward(k)
        for i in range(LO):
            total = acc[:, i]
            if k < 4:
                up_back(k + 1, i).wait_recv()
                total = total + up_in[k, i].astype(F32)
            stage[k, i] = total.astype(BF16)
            go(up_back(k, i))

    def send_down(k):
        backward(k)
        for i in range(LO):
            total = acc[:, i]
            if k > 5:
                down_back(k - 1, i).wait_recv()
                total = total + down_in[k - 6, i].astype(F32)
            stage[k, i] = total.astype(BF16)
            go(down_back(k, i))

    send_up(4)
    send_down(5)

    def part_copy(d):
        m = lax.rem(hi + d, N_HI) * 2 + 1 - core
        return copy(part.at[m], psib.at[d], part_send.at[d], part_recv.at[d], sibling)

    def far_copy(d):
        return copy(pmine.at[d], pfar.at[d], pfar_send.at[d], pfar_recv.at[d], at_hi(d))

    for m in range(N_HEAD):
        part[m] = mm(attended, w[:, m * WIDTH:(m + 1) * WIDTH]).astype(BF16)
    for d in (2, 1, 3, 0):
        go(part_copy(d))

    send_up(3)
    send_down(6)

    for d in (2, 1, 3, 0):
        part_copy(d).wait_recv()
        m = lax.rem(hi + d, N_HI) * 2 + core
        both = part[m].astype(F32) + psib[d].astype(F32)
        pmine[d] = both.astype(BF16)
        if d:
            go(far_copy(d))

    send_up(2)
    send_down(7)
    send_up(1)
    send_down(8)
    backward(0)
    for i in range(LO):
        up_back(1, i).wait_recv()
        down_back(8, i).wait_recv()
        zs[i] = (acc[:, i] + up_in[0, i].astype(F32) + down_in[3, i].astype(F32)).astype(BF16)

    def z_back(r):
        return copy(zs.at[lax.rem(z + r, LO)], zr.at[r - 1], z_send.at[r - 1], z_recv.at[r - 1], at_lo(r))

    for r in (1, 2):
        go(z_back(r))

    dq_t = mm(kt[...], p_buf[...]) * (inv * SCALE)
    dq_ref[...] = jnp.concatenate([dq_t[:, i * HD:(i + 1) * HD].T for i in range(GROUP)], axis=1).astype(BF16)

    for d in (1, 2, 3):
        far_copy(d).wait_recv()
    mixed_ref[...] = (
        pmine[0].astype(F32) + pfar[1].astype(F32) + pfar[2].astype(F32) + pfar[3].astype(F32)
    ).astype(BF16)

    for r in (1, 2):
        z_back(r).wait_recv()
    mine = zs[z].astype(F32) + zr[0].astype(F32) + zr[1].astype(F32)
    dk_ref[...] = mine[0].astype(BF16)
    dv_ref[...] = mine[1].astype(BF16)

    for c in sent:
        c.wait_send()


def shards(query_heads, key_heads, value_heads, out_weight, out_grad, clip_lengths):
    dma = pltpu.SemaphoreType.DMA
    vmem = pltpu.VMEM
    keys = (REACH + 1) * BUNDLE
    whole = pl.BlockSpec(memory_space=pltpu.VMEM)
    block = jax.ShapeDtypeStruct((TOK, WIDTH), BF16)
    small = jax.ShapeDtypeStruct((TOK, HD), BF16)
    piece = (2, TOK, HD)
    return pl.pallas_call(
        kernel,
        out_shape=(block, block, block, small, small),
        in_specs=[pl.BlockSpec(memory_space=pltpu.SMEM)] + [whole] * 4 + [pl.BlockSpec(memory_space=pl.ANY)],
        out_specs=[whole] * 5,
        scratch_shapes=[
            vmem((REACH + 1, LO) + piece, BF16),
            vmem((N_HEAD, TOK, WIDTH), BF16),
            vmem((WIDTH, N_HEAD * WIDTH), BF16),
            vmem((HD, WIDTH), BF16),
            vmem((WIDTH, HD), BF16),
            vmem((HD, WIDTH), BF16),
            vmem((WIDTH, HD), BF16),
            vmem((8, WIDTH), jnp.int32),
            vmem((REACH + 1, BUNDLE, WIDTH), F32),
            vmem((keys, WIDTH), BF16),
            vmem((HD, keys), BF16),
            vmem((HD, keys), BF16),
            vmem((8, WIDTH), F32),
            vmem((2, LO, TOK, HD), F32),
            vmem((N_HEAD, TOK, WIDTH), BF16),
            vmem((N_HI, TOK, WIDTH), BF16),
            vmem((N_HI, TOK, WIDTH), BF16),
            vmem((N_HI, TOK, WIDTH), BF16),
            vmem((4, LO) + piece, BF16),
            vmem((4, LO) + piece, BF16),
            vmem((REACH + 1, LO) + piece, BF16),
            vmem((LO,) + piece, BF16),
            vmem((LO - 1,) + piece, BF16),
            dma,
            dma((REACH + 1, LO)), dma((REACH + 1, LO)),
            dma((N_HI,)), dma((N_HI,)), dma((N_HI,)), dma((N_HI,)),
            dma((N_HI,)), dma((N_HI,)), dma((N_HI,)), dma((N_HI,)),
            dma((4, LO)), dma((4, LO)), dma((4, LO)), dma((4, LO)),
            dma((LO - 1,)), dma((LO - 1,)),
        ],
        compiler_params=pltpu.CompilerParams(
            collective_id=0, has_side_effects=True, vmem_limit_bytes=48 * 1024 * 1024
        ),
        cost_estimate=pl.CostEstimate(flops=3_000_000_000, bytes_accessed=4_000_000, transcendentals=1_400_000),
    )(clip_lengths, query_heads, key_heads, value_heads, out_grad, out_weight)


def solution(mesh):
    wide = P("seq", "head")
    return jax.shard_map(
        shards,
        mesh=mesh,
        in_specs=(wide, wide, wide, P("head", None), wide, P()),
        out_specs=(wide,) * 5,
        check_vma=False,
    )
```

```python
import math

import jax
import jax.numpy as jnp
from jax import lax
from jax.experimental import pallas as pl
from jax.experimental.pallas import tpu as pltpu
from jax.sharding import PartitionSpec as P

HD = 128
GROUP = 3
TOK = 128
LO = 3
LINKS = 32
RING = 8
N_SEQ = LO * LINKS
N_HEAD = 8
N_HI = 4
WIDTH = GROUP * HD
BUNDLE = LO * TOK
SCALE = 1.0 / math.sqrt(HD)
EXP2_SCALE = SCALE * math.log2(math.e)
MASKED = -1e30
MESH = pl.DeviceIdType.MESH
F32 = jnp.float32
BF16 = jnp.bfloat16


def mm(a, b):
    return jnp.dot(a, b, preferred_element_type=F32)


def mm_t(a, b):
    return lax.dot_general(a, b, (((1,), (1,)), ((), ())), preferred_element_type=F32)


def blocks_t(x):
    if x.shape[0] == HD:
        return jnp.concatenate([x[:, i * HD:(i + 1) * HD].T for i in range(GROUP)], axis=0)
    return jnp.concatenate([x[i * HD:(i + 1) * HD, :].T for i in range(GROUP)], axis=1)


def kernel(
    clip_ref, q_hbm, k_hbm, v_hbm, og_hbm, w_hbm,
    mixed_hbm, att_hbm, dq_hbm, dk_hbm, dv_hbm,
    q_in, kv, og, w, qt, qs, dot, dos, s_buf, p_buf, kt, vt, mx, acc,
    part, psib, pmine, pfar, up_in, down_in, stage, zs, zr,
    mixed_ref, att_ref, dq_ref, dk_ref, dv_ref,
    in_sem, out_sem, ready,
    kv_send, kv_recv, og_send, og_recv, osib_send, osib_recv,
    part_send, part_recv, pfar_send, pfar_recv,
    up_send, up_recv, down_send, down_recv, z_send, z_recv,
):
    s = lax.axis_index("seq")
    n = lax.axis_index("head")
    link, z = lax.div(s, LO), lax.rem(s, LO)
    hi, core = lax.div(n, 2), lax.rem(n, 2)
    y = lax.rem(link, RING)
    last, inner = y == RING - 1, y < RING - 1

    def at_seq(step):
        return (lax.rem(s + step + N_SEQ, N_SEQ), n)

    def at_link(step):
        return at_seq(step * LO)

    def at_lo(r):
        return (link * LO + lax.rem(z + r, LO), n)

    def at_hi(d):
        return (s, lax.rem(hi + d, N_HI) * 2 + core)

    sibling = (s, hi * 2 + 1 - core)
    lo_of = [lax.rem(z + LO - r, LO) for r in range(LO)]

    def copy(src, dst, ssem, rsem, dev):
        return pltpu.make_async_remote_copy(
            src_ref=src, dst_ref=dst, send_sem=ssem, recv_sem=rsem, device_id=dev, device_id_type=MESH
        )

    sent = []

    def go(c):
        c.start()
        sent.append(c)

    def go_if(cond, c):
        pl.when(cond)(c.start)

    def load(i, src, dst):
        c = pltpu.make_async_copy(src, dst, in_sem.at[i])
        c.start()
        return c

    loads = [
        load(0, k_hbm, kv.at[0, z, 0]), load(1, v_hbm, kv.at[0, z, 1]),
        load(2, og_hbm, og.at[n]), load(3, q_hbm, q_in), load(4, w_hbm, w),
    ]

    barrier = pltpu.get_barrier_semaphore()
    near = [at_link(1), at_link(-1), at_link(RING), at_link(-RING), at_lo(1), at_lo(2), sibling]
    for dev in near:
        pl.semaphore_signal(barrier, inc=1, device_id=dev, device_id_type=MESH)

    def greet(cond, dev, sem):
        @pl.when(cond)
        def _():
            pl.semaphore_signal(sem, inc=1, device_id=dev, device_id_type=MESH)

    greet(last, at_seq(-(RING - 1) * LO), barrier)
    greet(y == 0, at_seq((RING - 1) * LO), barrier)
    for d in (1, 2, 3):
        greet(hi + d < N_HI, at_hi(d), barrier)
    ends = jnp.where(last | (y == 0), 1, 0)
    pl.semaphore_wait(barrier, len(near) + hi + ends)
    for d in (1, 2, 3):
        greet(hi + d >= N_HI, at_hi(d), ready.at[N_HI - d])

    def z_copy(r):
        return copy(kv.at[0, z], kv.at[0, z], kv_send.at[0, r], kv_recv.at[0, r], at_lo(r))

    def up_copy(k, r):
        src, dev = k - 1, at_link(1)
        if k == 1 and r == 0:
            src = jnp.where(last, RING, 0)
            dev = at_seq(jnp.where(last, -(RING - 1) * LO, LO))
        return copy(kv.at[src, lo_of[r]], kv.at[k, lo_of[r]], kv_send.at[k, r], kv_recv.at[k, r], dev)

    def down_copy(k, r):
        src, dev = (0, at_link(RING)) if k == RING else (k + 1, at_link(-1))
        return copy(kv.at[src, lo_of[r]], kv.at[k, lo_of[r]], kv_send.at[k, r], kv_recv.at[k, r], dev)

    def og_copy(d):
        return copy(og.at[n], og.at[n], og_send.at[d], og_recv.at[d], at_hi(d))

    def sib_copy(d):
        m = lax.rem(hi + N_HI - d, N_HI) * 2 + core
        return copy(og.at[m], og.at[m], osib_send.at[d], osib_recv.at[d], sibling)

    loads[0].wait()
    loads[1].wait()
    go_if(inner, up_copy(1, 0))
    go(down_copy(RING, 0))
    for r in (1, 2):
        go(z_copy(r))
    loads[2].wait()
    for d in (1, 2, 3):
        go_if(hi + d >= N_HI, og_copy(d))
    go(sib_copy(0))

    loads[3].wait()
    qt[...] = jnp.concatenate(
        [q_in[:, i * HD:(i + 1) * HD].astype(F32).T for i in range(GROUP)], axis=1
    ).astype(BF16)
    lane = lax.broadcasted_iota(jnp.int32, (1, WIDTH), 1)
    pos = s * TOK + lax.rem(lane, TOK)
    begin = jnp.zeros_like(pos)
    end = jnp.int32(0)
    for i in range(8):
        end = end + clip_ref[i]
        begin = jnp.where(pos >= end, end, begin)

    def scores(k):
        sc = mm(kv[k, :, 0].reshape(BUNDLE, HD), qt[...])
        row = (link - k) * BUNDLE + lax.broadcasted_iota(jnp.int32, (BUNDLE, WIDTH), 0)
        ok = row >= begin
        if k == 0:
            ok = ok & (row <= pos)
        sc = jnp.where(ok, sc, MASKED)
        s_buf[k] = sc
        top = jnp.max(sc.reshape(BUNDLE // 8, 8, WIDTH), axis=0)
        mx[...] = top if k == 0 else jnp.maximum(mx[...], top)
        for i in range(LO):
            cols = slice(k * BUNDLE + i * TOK, k * BUNDLE + (i + 1) * TOK)
            kt[:, cols] = kv[k, i, 0].T
            vt[:, cols] = kv[k, i, 1].T

    def down_step(k, r):
        down_copy(k, r).wait_recv()
        if k > (4 if r == 0 else 5):
            go(down_copy(k - 1, r))
        if k == RING and r == 0:
            go_if(last, up_copy(1, 0))

    def up_step(k, r):
        up_copy(k, r).wait_recv()
        if k < (3 if r == 0 else 4):
            go(up_copy(k + 1, r))

    def og_up(d):
        @pl.when(hi + d < N_HI)
        def _():
            pl.semaphore_wait(ready.at[d], 1)
            og_copy(d).start()

    down_step(8, 0)
    for r in (1, 2):
        z_copy(r).wait_recv()
        go(up_copy(1, r))
        go(down_copy(RING, r))
    up_step(1, 0)
    sent.append(up_copy(1, 0))
    scores(0)
    down_step(7, 0)
    up_step(2, 0)
    for r in (1, 2):
        down_step(8, r)
        up_step(1, r)
    og_up(1)
    down_step(6, 0)
    scores(8)
    scores(1)
    up_step(3, 0)
    for r in (1, 2):
        down_step(7, r)
        up_step(2, r)
    down_step(5, 0)
    og_up(2)
    og_up(3)
    scores(7)
    scores(2)
    for r in (1, 2):
        down_step(6, r)
        up_step(3, r)
    down_step(4, 0)
    scores(6)
    scores(3)
    for r in (1, 2):
        down_step(5, r)
        up_step(4, r)
    scores(5)
    scores(4)

    top = jnp.max(mx[...], axis=0, keepdims=True) * EXP2_SCALE
    total = jnp.zeros((8, WIDTH), F32)
    for k in range(RING + 1):
        p = jnp.exp2(s_buf[k] * EXP2_SCALE - top)
        total = total + jnp.sum(p.reshape(BUNDLE // 8, 8, WIDTH), axis=0)
        p_buf[k * BUNDLE:(k + 1) * BUNDLE, :] = p.astype(BF16)
    inv = 1.0 / jnp.sum(total, axis=0, keepdims=True)
    out_t = (mm(vt[...], p_buf[...]) * inv).astype(BF16).astype(F32)
    attended = jnp.concatenate([out_t[:, i * HD:(i + 1) * HD].T for i in range(GROUP)], axis=1).astype(BF16)
    att_ref[...] = attended

    def store(i, src, dst):
        c = pltpu.make_async_copy(src, dst, out_sem.at[i])
        c.start()
        return c

    stores = [store(0, att_ref, att_hbm)]

    for d in (3, 2, 1):
        og_copy(d).wait_recv()
        go(sib_copy(d))
    loads[4].wait()
    for d in (0, 3, 2, 1):
        sib_copy(d).wait_recv()
    dh = mm_t(w[:, 0:WIDTH], og[0])
    for m in range(1, N_HEAD):
        dh = dh + mm_t(w[:, m * WIDTH:(m + 1) * WIDTH], og[m])
    d_t = jnp.concatenate([dh[i * HD:(i + 1) * HD, :] for i in range(GROUP)], axis=1).astype(BF16)
    dot[...] = d_t
    d_t = d_t.astype(F32)
    delta = jnp.sum(d_t * out_t, axis=0, keepdims=True)
    dos[...] = blocks_t(d_t * inv).astype(BF16)
    qs[...] = blocks_t(qt[...].astype(F32) * (inv * SCALE)).astype(BF16)

    def backward(k):
        rows = slice(k * BUNDLE, (k + 1) * BUNDLE)
        p = p_buf[rows, :]
        dp = mm(kv[k, :, 1].reshape(BUNDLE, HD), dot[...])
        ds = (p.astype(F32) * (dp - delta)).astype(BF16)
        dv = mm(p, dos[...])
        dk = mm(ds, qs[...])
        for i in range(LO):
            acc[k, i, 0] = dk[i * TOK:(i + 1) * TOK, :]
            acc[k, i, 1] = dv[i * TOK:(i + 1) * TOK, :]
        p_buf[rows, :] = ds

    back = [lax.rem(z + r, LO) for r in range(LO)]
    order = (1, 2, 0)

    def up_back(k, r):
        dev = at_link(-1)
        if k == 1 and r == 1:
            dev = at_seq(jnp.where(y == 0, (RING - 1) * LO, -LO))
        return copy(stage.at[k, back[r]], up_in.at[k - 1, back[r]], up_send.at[k - 1, r], up_recv.at[k - 1, r], dev)

    def down_back(k, r):
        dev = at_link(-RING) if k == RING else at_link(1)
        src = stage.at[9 if k == 4 else k, back[r]]
        return copy(src, down_in.at[k - 4, back[r]], down_send.at[k - 4, r], down_recv.at[k - 4, r], dev)

    def mine(k, r):
        return acc[k, back[r]]

    def send_up(k, r):
        total = mine(k, r)
        if k < (3 if r == 1 else 4):
            up_back(k + 1, r).wait_recv()
            total = total + up_in[k, back[r]].astype(F32)
        stage[k, back[r]] = total.astype(BF16)
        go(up_back(k, r))

    def send_down(k, r):
        total = mine(k, r)
        if k > (4 if r == 1 else 5):
            down_back(k - 1, r).wait_recv()
            total = total + down_in[k - 5, back[r]].astype(F32)
        if k == RING and r == 1:

            @pl.when(last)
            def _():
                up_back(1, 1).wait_recv()
                stage[RING, back[1]] = (total + up_in[0, back[1]].astype(F32)).astype(BF16)

            @pl.when(inner)
            def _():
                stage[RING, back[1]] = total.astype(BF16)
        else:
            stage[9 if k == 4 else k, back[r]] = total.astype(BF16)
        go(down_back(k, r))

    backward(4)
    send_down(4, 1)
    send_up(4, 2)
    send_up(4, 0)
    backward(5)
    send_down(5, 2)
    send_down(5, 0)
    backward(3)
    send_up(3, 1)

    def part_copy(d):
        m = lax.rem(hi + d, N_HI) * 2 + 1 - core
        return copy(part.at[m], psib.at[d], part_send.at[d], part_recv.at[d], sibling)

    def far_copy(d):
        return copy(pmine.at[d], pfar.at[d], pfar_send.at[d], pfar_recv.at[d], at_hi(d))

    for m in range(N_HEAD):
        part[m] = mm(attended, w[:, m * WIDTH:(m + 1) * WIDTH]).astype(BF16)
    for d in (1, 2, 3, 0):
        go(part_copy(d))
    backward(6)
    send_down(5, 1)
    for r in (2, 0):
        send_up(3, r)
        send_down(6, r)
    send_down(6, 1)

    for d in (1, 2, 3, 0):
        part_copy(d).wait_recv()
        m = lax.rem(hi + d, N_HI) * 2 + core
        both = part[m].astype(F32) + psib[d].astype(F32)
        pmine[d] = both.astype(BF16)
        if d:
            go(far_copy(d))

    backward(2)
    backward(7)
    send_up(2, 1)
    for r in (2, 0):
        send_up(2, r)
        send_down(7, r)
    send_down(7, 1)
    backward(1)
    backward(8)
    send_up(1, 1)
    for r in (2, 0):
        send_up(1, r)
        send_down(8, r)
    send_down(8, 1)
    backward(0)

    def z_back(r):
        return copy(zs.at[back[r]], zr.at[r - 1], z_send.at[r - 1], z_recv.at[r - 1], at_lo(r))

    def final(r):
        total = mine(0, r)
        if r == 1:

            @pl.when(inner)
            def _():
                up_back(1, 1).wait_recv()
                acc[0, back[1]] = total + up_in[0, back[1]].astype(F32)

            total = mine(0, r)
        else:
            up_back(1, r).wait_recv()
            total = total + up_in[0, back[r]].astype(F32)
        down_back(8, r).wait_recv()
        total = total + down_in[4, back[r]].astype(F32)
        if r:
            zs[back[r]] = total.astype(BF16)
            go(z_back(r))
        return total

    final(2)
    own = final(0)
    final(1)

    dq_t = mm(kt[...], p_buf[...]) * (inv * SCALE)
    dq_ref[...] = jnp.concatenate([dq_t[:, i * HD:(i + 1) * HD].T for i in range(GROUP)], axis=1).astype(BF16)
    stores.append(store(1, dq_ref, dq_hbm))

    for d in (1, 2, 3):
        far_copy(d).wait_recv()
    mixed_ref[...] = (
        pmine[0].astype(F32) + pfar[1].astype(F32) + pfar[2].astype(F32) + pfar[3].astype(F32)
    ).astype(BF16)
    stores.append(store(2, mixed_ref, mixed_hbm))

    for r in (1, 2):
        z_back(r).wait_recv()
    own = own + zr[0].astype(F32) + zr[1].astype(F32)
    dk_ref[...] = own[0].astype(BF16)
    dv_ref[...] = own[1].astype(BF16)
    stores.append(store(3, dk_ref, dk_hbm))
    stores.append(store(4, dv_ref, dv_hbm))

    for d in (1, 2, 3):
        sent.append(og_copy(d))
    for c in sent:
        c.wait_send()
    for c in stores:
        c.wait()


def finish(*refs):
    sources, targets, sem = refs[:5], refs[5:10], refs[10]
    copies = [pltpu.make_async_copy(a, b, sem.at[i]) for i, (a, b) in enumerate(zip(sources, targets))]
    for c in copies:
        c.start()
    for c in copies:
        c.wait()


def shards(query_heads, key_heads, value_heads, out_weight, out_grad, clip_lengths):
    dma = pltpu.SemaphoreType.DMA
    vmem = pltpu.VMEM
    keys = (RING + 1) * BUNDLE
    hbm = pl.BlockSpec(memory_space=pl.ANY)
    block = jax.ShapeDtypeStruct((TOK, WIDTH), BF16)
    small = jax.ShapeDtypeStruct((TOK, HD), BF16)
    shapes = (block, block, block, small, small)
    piece = (2, TOK, HD)
    results = pl.pallas_call(
        kernel,
        out_shape=shapes,
        in_specs=[pl.BlockSpec(memory_space=pltpu.SMEM)] + [hbm] * 5,
        out_specs=[hbm] * 5,
        scratch_shapes=[
            vmem((TOK, WIDTH), BF16),
            vmem((RING + 1, LO) + piece, BF16),
            vmem((N_HEAD, TOK, WIDTH), BF16),
            vmem((WIDTH, N_HEAD * WIDTH), BF16),
            vmem((HD, WIDTH), BF16),
            vmem((WIDTH, HD), BF16),
            vmem((HD, WIDTH), BF16),
            vmem((WIDTH, HD), BF16),
            vmem((RING + 1, BUNDLE, WIDTH), F32),
            vmem((keys, WIDTH), BF16),
            vmem((HD, keys), BF16),
            vmem((HD, keys), BF16),
            vmem((8, WIDTH), F32),
            vmem((RING + 1, LO) + piece, F32),
            vmem((N_HEAD, TOK, WIDTH), BF16),
            vmem((N_HI, TOK, WIDTH), BF16),
            vmem((N_HI, TOK, WIDTH), BF16),
            vmem((N_HI, TOK, WIDTH), BF16),
            vmem((4, LO) + piece, BF16),
            vmem((5, LO) + piece, BF16),
            vmem((RING + 2, LO) + piece, BF16),
            vmem((LO,) + piece, BF16),
            vmem((LO - 1,) + piece, BF16),
            vmem((TOK, WIDTH), BF16), vmem((TOK, WIDTH), BF16), vmem((TOK, WIDTH), BF16),
            vmem((TOK, HD), BF16), vmem((TOK, HD), BF16),
            dma((5,)), dma((5,)), pltpu.SemaphoreType.REGULAR((N_HI,)),
            dma((RING + 1, LO)), dma((RING + 1, LO)),
            dma((N_HI,)), dma((N_HI,)), dma((N_HI,)), dma((N_HI,)),
            dma((N_HI,)), dma((N_HI,)), dma((N_HI,)), dma((N_HI,)),
            dma((4, LO)), dma((4, LO)), dma((5, LO)), dma((5, LO)),
            dma((LO - 1,)), dma((LO - 1,)),
        ],
        compiler_params=pltpu.CompilerParams(
            collective_id=0, has_side_effects=True, vmem_limit_bytes=60 * 1024 * 1024
        ),
        cost_estimate=pl.CostEstimate(flops=3_000_000_000, bytes_accessed=4_000_000, transcendentals=1_400_000),
    )(clip_lengths, query_heads, key_heads, value_heads, out_grad, out_weight)
    return pl.pallas_call(
        finish,
        out_shape=shapes,
        in_specs=[hbm] * 5,
        out_specs=[hbm] * 5,
        scratch_shapes=[dma((5,))],
    )(*results)


def solution(mesh):
    wide = P("seq", "head")
    return jax.shard_map(
        shards,
        mesh=mesh,
        in_specs=(wide, wide, wide, P("head", None), wide, P()),
        out_specs=(wide,) * 5,
        check_vma=False,
    )
```

```python
import math

import jax
import jax.numpy as jnp
from jax import lax
from jax.experimental import pallas as pl
from jax.experimental.pallas import tpu as pltpu
from jax.sharding import PartitionSpec as P

HD = 128
GROUP = 3
TOK = 128
LO = 3
LINKS = 32
RING = 8
N_SEQ = LO * LINKS
N_HEAD = 8
N_HI = 4
WIDTH = GROUP * HD
BUNDLE = LO * TOK
SCALE = 1.0 / math.sqrt(HD)
EXP2_SCALE = SCALE * math.log2(math.e)
MASKED = -1e30
MESH = pl.DeviceIdType.MESH
F32 = jnp.float32
BF16 = jnp.bfloat16


def mm(a, b):
    return jnp.dot(a, b, preferred_element_type=F32)


def mm_t(a, b):
    return lax.dot_general(a, b, (((1,), (1,)), ((), ())), preferred_element_type=F32)


def blocks_t(x):
    if x.shape[0] == HD:
        return jnp.concatenate([x[:, i * HD:(i + 1) * HD].T for i in range(GROUP)], axis=0)
    return jnp.concatenate([x[i * HD:(i + 1) * HD, :].T for i in range(GROUP)], axis=1)


def kernel(
    clip_ref, q_hbm, k_hbm, v_hbm, og_hbm, w_hbm,
    mixed_hbm, att_hbm, dq_hbm, dk_hbm, dv_hbm,
    q_in, kv, og, w, qt, qs, dot, dos, s_buf, p_buf, kt, vt, mx, acc,
    part, psib, pmine, pfar, come, mate, stage,
    mixed_ref, att_ref, dq_ref, dk_ref, dv_ref,
    in_sem, out_sem, ready,
    kv_send, kv_recv, lo_send, lo_recv, og_send, og_recv, osib_send, osib_recv,
    part_send, part_recv, pfar_send, pfar_recv,
    up_send, up_recv, z_send, z_recv,
):
    s = lax.axis_index("seq")
    n = lax.axis_index("head")
    link, z = lax.div(s, LO), lax.rem(s, LO)
    hi, core = lax.div(n, 2), lax.rem(n, 2)
    y = lax.rem(link, RING)
    first, last = y == 0, y == RING - 1
    not_first, not_last = y > 0, y < RING - 1

    def at_seq(step):
        return (lax.rem(s + step + N_SEQ, N_SEQ), n)

    def at_link(step):
        return at_seq(step * LO)

    def at_lo(r):
        return (link * LO + lax.rem(z + r, LO), n)

    def at_hi(d):
        return (s, lax.rem(hi + d, N_HI) * 2 + core)

    sibling = (s, hi * 2 + 1 - core)
    lo_of = [lax.rem(z + LO - r, LO) for r in range(LO)]

    def copy(src, dst, ssem, rsem, dev):
        return pltpu.make_async_remote_copy(
            src_ref=src, dst_ref=dst, send_sem=ssem, recv_sem=rsem, device_id=dev, device_id_type=MESH
        )

    sent = []

    def go(c):
        c.start()
        sent.append((None, c))

    def go_if(cond, c):
        pl.when(cond)(c.start)
        sent.append((cond, c))

    def load(i, src, dst):
        c = pltpu.make_async_copy(src, dst, in_sem.at[i])
        c.start()
        return c

    loads = [
        load(0, k_hbm, kv.at[0, z, 0]), load(1, v_hbm, kv.at[0, z, 1]),
        load(2, og_hbm, og.at[n]), load(3, q_hbm, q_in), load(4, w_hbm, w),
    ]

    barrier = pltpu.get_barrier_semaphore()
    near = [at_link(step * sign) for step in (1, 2, 6, RING) for sign in (1, -1)]
    near += [at_lo(1), at_lo(2), sibling]
    for dev in near:
        pl.semaphore_signal(barrier, inc=1, device_id=dev, device_id_type=MESH)

    def greet(cond, dev, sem):
        @pl.when(cond)
        def _():
            pl.semaphore_signal(sem, inc=1, device_id=dev, device_id_type=MESH)

    for d in (1, 2, 3):
        greet(hi + d < N_HI, at_hi(d), barrier)
    wrap = (RING - 1) * LO
    greet(first, at_seq(wrap), barrier)
    greet(last, at_seq(-wrap), barrier)
    pl.semaphore_wait(barrier, len(near) + hi + jnp.where(first | last, 1, 0))
    for d in (1, 2, 3):
        greet(hi + d >= N_HI, at_hi(d), ready.at[N_HI - d])

    def way(k, r):
        return {1: 1, 2: 1 if r else 2, 3: 1, 4: -2, 5: -1, 6: -1 if r else 6, 7: -1, RING: RING}[k]

    def move(k, r):
        step = way(k, r)
        return copy(
            kv.at[k - step, lo_of[r]], kv.at[k, lo_of[r]], kv_send.at[k, r], kv_recv.at[k, r], at_link(step)
        )

    def wrapped():
        return copy(kv.at[RING, z], kv.at[1, z], kv_send.at[1, 0], kv_recv.at[1, 0], at_seq(-wrap))

    def shared(r):
        return copy(kv.at[RING, z], kv.at[RING, z], kv_send.at[RING, r], kv_recv.at[RING, r], at_lo(r))

    def spread(k, r):
        return copy(kv.at[k, z], kv.at[k, z], lo_send.at[k, r], lo_recv.at[k, r], at_lo(r))

    def og_copy(d):
        return copy(og.at[n], og.at[n], og_send.at[d], og_recv.at[d], at_hi(d))

    def sib_copy(d):
        m = lax.rem(hi + N_HI - d, N_HI) * 2 + core
        return copy(og.at[m], og.at[m], osib_send.at[d], osib_recv.at[d], sibling)

    loads[0].wait()
    loads[1].wait()
    go(move(RING, 0))
    go(move(6, 0))
    go(move(2, 0))
    go_if(not_last, move(1, 0))
    for r in (1, 2):
        go(spread(0, r))
    loads[3].wait()
    qt[...] = jnp.concatenate(
        [q_in[:, i * HD:(i + 1) * HD].astype(F32).T for i in range(GROUP)], axis=1
    ).astype(BF16)
    lane = lax.broadcasted_iota(jnp.int32, (1, WIDTH), 1)
    pos = s * TOK + lax.rem(lane, TOK)
    begin = jnp.zeros_like(pos)
    end = jnp.int32(0)
    for i in range(8):
        end = end + clip_ref[i]
        begin = jnp.where(pos >= end, end, begin)

    def scores(k):
        sc = mm(kv[k, :, 0].reshape(BUNDLE, HD), qt[...])
        row = (link - k) * BUNDLE + lax.broadcasted_iota(jnp.int32, (BUNDLE, WIDTH), 0)
        ok = row >= begin
        if k == 0:
            ok = ok & (row <= pos)
        sc = jnp.where(ok, sc, MASKED)
        s_buf[k] = sc
        top = jnp.max(sc.reshape(BUNDLE // 8, 8, WIDTH), axis=0)
        mx[...] = top if k == 0 else jnp.maximum(mx[...], top)
        for i in range(LO):
            cols = slice(k * BUNDLE + i * TOK, k * BUNDLE + (i + 1) * TOK)
            kt[:, cols] = kv[k, i, 0].T
            vt[:, cols] = kv[k, i, 1].T

    def og_up(d):
        @pl.when(hi + d < N_HI)
        def _():
            pl.semaphore_wait(ready.at[d], 1)
            og_copy(d).start()

    def got(k, r, *then):
        move(k, r).wait_recv()
        for c in then:
            go(c)

    got(6, 0, move(5, 0), move(4, 0))
    got(2, 0, move(3, 0))
    got(RING, 0, move(7, 0))
    go_if(last, wrapped())
    for r in (1, 2):
        go_if(first, shared(r))
    for r in (1, 2):
        spread(0, r).wait_recv()
        go(move(1, r))
        go_if(not_first, move(RING, r))
    loads[2].wait()
    for d in (1, 2, 3):
        go_if(hi + d >= N_HI, og_copy(d))
    go(sib_copy(0))
    got(1, 0)
    scores(0)
    got(5, 0, spread(5, 1), spread(5, 2))
    for r in (1, 2):
        got(RING, r, move(7, r))
        got(1, r, move(2, r))
    got(4, 0, spread(4, 1), spread(4, 2))
    got(7, 0)
    got(3, 0)
    og_up(1)
    scores(1)
    scores(RING)
    for r in (1, 2):
        got(7, r, move(6, r))
        got(2, r, move(3, r))
    scores(2)
    scores(7)
    for k in (5, 4):
        for r in (1, 2):
            spread(k, r).wait_recv()
        scores(k)
    for k in (6, 3):
        for r in (1, 2):
            got(k, r)
        scores(k)
    og_up(2)
    og_up(3)

    top = jnp.max(mx[...], axis=0, keepdims=True) * EXP2_SCALE
    total = jnp.zeros((8, WIDTH), F32)
    for k in range(RING + 1):
        p = jnp.exp2(s_buf[k] * EXP2_SCALE - top)
        total = total + jnp.sum(p.reshape(BUNDLE // 8, 8, WIDTH), axis=0)
        p_buf[k * BUNDLE:(k + 1) * BUNDLE, :] = p.astype(BF16)
    inv = 1.0 / jnp.sum(total, axis=0, keepdims=True)
    out_t = (mm(vt[...], p_buf[...]) * inv).astype(BF16).astype(F32)
    attended = jnp.concatenate([out_t[:, i * HD:(i + 1) * HD].T for i in range(GROUP)], axis=1).astype(BF16)
    att_ref[...] = attended

    def store(i, src, dst):
        c = pltpu.make_async_copy(src, dst, out_sem.at[i])
        c.start()
        return c

    stores = [store(0, att_ref, att_hbm)]

    def part_copy(d):
        m = lax.rem(hi + d, N_HI) * 2 + 1 - core
        return copy(part.at[m], psib.at[d], part_send.at[d], part_recv.at[d], sibling)

    def far_copy(d):
        return copy(pmine.at[d], pfar.at[d], pfar_send.at[d], pfar_recv.at[d], at_hi(d))

    loads[4].wait()
    for d in (1, 2, 3, 0):
        m = lax.rem(hi + d, N_HI) * 2 + 1 - core
        part[m] = mm(attended, w[:, pl.ds(pl.multiple_of(m * WIDTH, HD), WIDTH)]).astype(BF16)
        go(part_copy(d))
    for d in (1, 2, 3, 0):
        m = lax.rem(hi + d, N_HI) * 2 + core
        part[m] = mm(attended, w[:, pl.ds(pl.multiple_of(m * WIDTH, HD), WIDTH)]).astype(BF16)
    for d in (1, 2, 3, 0):
        part_copy(d).wait_recv()
        m = lax.rem(hi + d, N_HI) * 2 + core
        both = part[m].astype(F32) + psib[d].astype(F32)
        pmine[d] = both.astype(BF16)
        if d:
            go(far_copy(d))

    for d in (3, 2, 1):
        og_copy(d).wait_recv()
        go(sib_copy(d))
    for d in (0, 3, 2, 1):
        sib_copy(d).wait_recv()
    dh = mm_t(w[:, 0:WIDTH], og[0])
    for m in range(1, N_HEAD):
        dh = dh + mm_t(w[:, m * WIDTH:(m + 1) * WIDTH], og[m])
    d_t = jnp.concatenate([dh[i * HD:(i + 1) * HD, :] for i in range(GROUP)], axis=1).astype(BF16)
    dot[...] = d_t
    d_t = d_t.astype(F32)
    delta = jnp.sum(d_t * out_t, axis=0, keepdims=True)
    dos[...] = blocks_t(d_t * inv).astype(BF16)
    qs[...] = blocks_t(qt[...].astype(F32) * (inv * SCALE)).astype(BF16)

    def backward(k):
        rows = slice(k * BUNDLE, (k + 1) * BUNDLE)
        p = p_buf[rows, :]
        dp = mm(kv[k, :, 1].reshape(BUNDLE, HD), dot[...])
        ds = (p.astype(F32) * (dp - delta)).astype(BF16)
        dv = mm(p, dos[...])
        dk = mm(ds, qs[...])
        for i in range(LO):
            acc[k, i, 0] = dk[i * TOK:(i + 1) * TOK, :]
            acc[k, i, 1] = dv[i * TOK:(i + 1) * TOK, :]
        p_buf[rows, :] = ds

    back = [lax.rem(z + r, LO) for r in range(LO)]

    def give(k, r):
        step = way(k, r)
        return copy(stage.at[k, back[r]], come.at[k, back[r]], up_send.at[k, r], up_recv.at[k, r], at_link(-step))

    def give_wrapped():
        return copy(stage.at[1, z], come.at[1, z], up_send.at[1, 0], up_recv.at[1, 0], at_seq(wrap))

    def gather(k, r):
        return copy(stage.at[k, back[r]], mate.at[k, r], z_send.at[k, r], z_recv.at[k, r], at_lo(r))

    def fill(k, r, *terms):
        total = acc[k, back[r]]
        for t in terms:
            total = total + t.astype(F32)
        stage[k, back[r]] = total.astype(BF16)

    def send(c, k, r, *terms):
        fill(k, r, *terms)
        go(c)

    def came(k, r):
        give(k, r).wait_recv()
        return come[k, back[r]]

    def mates(k):
        for r in (1, 2):
            gather(k, r).wait_recv()
        return mate[k, 1].astype(F32) + mate[k, 2].astype(F32)

    backward(3)
    for r in (1, 2, 0):
        send(give(3, r), 3, r)
    backward(6)
    for r in (1, 2):
        send(give(6, r), 6, r)
    for k in (4, 5):
        backward(k)
        for r in (1, 2):
            send(gather(k, r), k, r)
    backward(7)
    send(give(7, 0), 7, 0)
    backward(2)

    for r in (1, 2):
        send(give(2, r), 2, r, came(3, r))
        send(give(7, r), 7, r, came(6, r))
    send(give(4, 0), 4, 0, mates(4))
    send(give(5, 0), 5, 0, mates(5))
    send(give(2, 0), 2, 0, came(3, 0))

    backward(RING)
    backward(1)
    fill(1, 0)
    go_if(not_first, give(1, 0))
    go_if(first, give_wrapped())
    for r in (1, 2):
        send(give(1, r), 1, r, came(2, r))
        fill(RING, r, came(7, r))
        go_if(not_first, give(RING, r))
        go_if(first, gather(RING, r))
    send(give(6, 0), 6, 0, came(4, 0), came(5, 0))

    @pl.when(first)
    def _():
        fill(RING, 0, came(7, 0), mates(RING))

    @pl.when(last)
    def _():
        fill(RING, 0, came(7, 0), came(1, 0))

    @pl.when(not_first & not_last)
    def _():
        fill(RING, 0, came(7, 0))

    go(give(RING, 0))
    backward(0)
    for r in (1, 2):

        @pl.when(first)
        def _():
            fill(0, r, came(1, r))

        @pl.when(not_first)
        def _():
            fill(0, r, came(1, r), came(RING, r))

        go(gather(0, r))

    dq_t = mm(kt[...], p_buf[...]) * (inv * SCALE)
    dq_ref[...] = jnp.concatenate([dq_t[:, i * HD:(i + 1) * HD].T for i in range(GROUP)], axis=1).astype(BF16)
    stores.append(store(1, dq_ref, dq_hbm))

    for d in (1, 2, 3):
        far_copy(d).wait_recv()
    mixed_ref[...] = (
        pmine[0].astype(F32) + pfar[1].astype(F32) + pfar[2].astype(F32) + pfar[3].astype(F32)
    ).astype(BF16)
    stores.append(store(2, mixed_ref, mixed_hbm))

    @pl.when(not_last)
    def _():
        acc[0, z] = acc[0, z] + came(1, 0).astype(F32)

    own = acc[0, z]
    for k in (2, 6, RING):
        own = own + came(k, 0).astype(F32)
    own = own + mates(0)
    dk_ref[...] = own[0].astype(BF16)
    dv_ref[...] = own[1].astype(BF16)
    stores.append(store(3, dk_ref, dk_hbm))
    stores.append(store(4, dv_ref, dv_hbm))

    for d in (1, 2, 3):
        sent.append((hi + d < N_HI, og_copy(d)))
    for cond, c in sent:
        c.wait_send() if cond is None else pl.when(cond)(c.wait_send)
    for c in stores:
        c.wait()


def finish(*refs):
    for source, target in zip(refs[:5], refs[5:]):
        target[...] = source[...]


def shards(query_heads, key_heads, value_heads, out_weight, out_grad, clip_lengths):
    dma = pltpu.SemaphoreType.DMA
    vmem = pltpu.VMEM
    keys = (RING + 1) * BUNDLE
    hbm = pl.BlockSpec(memory_space=pl.ANY)
    block = jax.ShapeDtypeStruct((TOK, WIDTH), BF16)
    small = jax.ShapeDtypeStruct((TOK, HD), BF16)
    shapes = (block, block, block, small, small)
    piece = (2, TOK, HD)
    results = pl.pallas_call(
        kernel,
        out_shape=shapes,
        in_specs=[pl.BlockSpec(memory_space=pltpu.SMEM)] + [hbm] * 5,
        out_specs=[hbm] * 5,
        scratch_shapes=[
            vmem((TOK, WIDTH), BF16),
            vmem((RING + 1, LO) + piece, BF16),
            vmem((N_HEAD, TOK, WIDTH), BF16),
            vmem((WIDTH, N_HEAD * WIDTH), BF16),
            vmem((HD, WIDTH), BF16),
            vmem((WIDTH, HD), BF16),
            vmem((HD, WIDTH), BF16),
            vmem((WIDTH, HD), BF16),
            vmem((RING + 1, BUNDLE, WIDTH), F32),
            vmem((keys, WIDTH), BF16),
            vmem((HD, keys), BF16),
            vmem((HD, keys), BF16),
            vmem((8, WIDTH), F32),
            vmem((RING + 1, LO) + piece, F32),
            vmem((N_HEAD, TOK, WIDTH), BF16),
            vmem((N_HI, TOK, WIDTH), BF16),
            vmem((N_HI, TOK, WIDTH), BF16),
            vmem((N_HI, TOK, WIDTH), BF16),
            vmem((RING + 1, LO) + piece, BF16),
            vmem((RING + 1, LO) + piece, BF16),
            vmem((RING + 1, LO) + piece, BF16),
            vmem((TOK, WIDTH), BF16), vmem((TOK, WIDTH), BF16), vmem((TOK, WIDTH), BF16),
            vmem((TOK, HD), BF16), vmem((TOK, HD), BF16),
            dma((5,)), dma((5,)), pltpu.SemaphoreType.REGULAR((N_HI,)),
            dma((RING + 1, LO)), dma((RING + 1, LO)), dma((RING + 1, LO)), dma((RING + 1, LO)),
            dma((N_HI,)), dma((N_HI,)), dma((N_HI,)), dma((N_HI,)),
            dma((N_HI,)), dma((N_HI,)), dma((N_HI,)), dma((N_HI,)),
            dma((RING + 1, LO)), dma((RING + 1, LO)), dma((RING + 1, LO)), dma((RING + 1, LO)),
        ],
        compiler_params=pltpu.CompilerParams(
            collective_id=0, has_side_effects=True, vmem_limit_bytes=60 * 1024 * 1024
        ),
        cost_estimate=pl.CostEstimate(flops=3_000_000_000, bytes_accessed=4_000_000, transcendentals=1_400_000),
    )(clip_lengths, query_heads, key_heads, value_heads, out_grad, out_weight)
    return pl.pallas_call(
        finish,
        out_shape=shapes,
        in_specs=[pl.BlockSpec(memory_space=pltpu.VMEM)] * 5,
        out_specs=[pl.BlockSpec(memory_space=pltpu.VMEM)] * 5,
        compiler_params=pltpu.CompilerParams(vmem_limit_bytes=60 * 1024 * 1024),
    )(*results)


def solution(mesh):
    wide = P("seq", "head")
    return jax.shard_map(
        shards,
        mesh=mesh,
        in_specs=(wide, wide, wide, P("head", None), wide, P()),
        out_specs=(wide,) * 5,
        check_vma=False,
    )
```

```python
import math

import jax
import jax.numpy as jnp
from jax import lax
from jax.experimental import pallas as pl
from jax.experimental.pallas import tpu as pltpu
from jax.sharding import PartitionSpec as P

HD = 128
GROUP = 3
TOK = 128
LO = 3
LINKS = 32
RING = 8
N_SEQ = LO * LINKS
N_HEAD = 8
N_HI = 4
WIDTH = GROUP * HD
BUNDLE = LO * TOK
SCALE = 1.0 / math.sqrt(HD)
EXP2_SCALE = SCALE * math.log2(math.e)
MASKED = -1e30
MESH = pl.DeviceIdType.MESH
F32 = jnp.float32
BF16 = jnp.bfloat16


def mm(a, b):
    return jnp.dot(a, b, preferred_element_type=F32)


def mm_t(a, b):
    return lax.dot_general(a, b, (((1,), (1,)), ((), ())), preferred_element_type=F32)


def blocks_t(x):
    if x.shape[0] == HD:
        return jnp.concatenate([x[:, i * HD:(i + 1) * HD].T for i in range(GROUP)], axis=0)
    return jnp.concatenate([x[i * HD:(i + 1) * HD, :].T for i in range(GROUP)], axis=1)


def kernel(
    clip_ref, q_hbm, k_hbm, v_hbm, og_hbm, w_hbm,
    mixed_hbm, att_hbm, dq_hbm, dk_hbm, dv_hbm,
    q_in, kv, og, w, qt, qs, dot, dos, s_buf, p_buf, kt, vt, mx, acc,
    part, psib, pmine, pfar, come, mate, stage,
    mixed_ref, att_ref, dq_ref, dk_ref, dv_ref,
    in_sem, out_sem, ready,
    kv_send, kv_recv, lo_send, lo_recv, og_send, og_recv, osib_send, osib_recv,
    part_send, part_recv, pfar_send, pfar_recv,
    up_send, up_recv, z_send, z_recv,
):
    s = lax.axis_index("seq")
    n = lax.axis_index("head")
    link, z = lax.div(s, LO), lax.rem(s, LO)
    hi, core = lax.div(n, 2), lax.rem(n, 2)
    y = lax.rem(link, RING)
    first, last = y == 0, y == RING - 1
    not_first, not_last = y > 0, y < RING - 1

    def at_seq(step):
        return (lax.rem(s + step + N_SEQ, N_SEQ), n)

    def at_link(step):
        return at_seq(step * LO)

    def at_lo(r):
        return (link * LO + lax.rem(z + r, LO), n)

    def at_hi(d):
        return (s, lax.rem(hi + d, N_HI) * 2 + core)

    sibling = (s, hi * 2 + 1 - core)
    lo_of = [lax.rem(z + LO - r, LO) for r in range(LO)]

    def copy(src, dst, ssem, rsem, dev):
        return pltpu.make_async_remote_copy(
            src_ref=src, dst_ref=dst, send_sem=ssem, recv_sem=rsem, device_id=dev, device_id_type=MESH
        )

    sent = []

    def go(c):
        c.start()
        sent.append((None, c))

    def go_if(cond, c):
        pl.when(cond)(c.start)
        sent.append((cond, c))

    def load(i, src, dst):
        c = pltpu.make_async_copy(src, dst, in_sem.at[i])
        c.start()
        return c

    loads = [
        load(0, k_hbm, kv.at[0, z, 0]), load(1, v_hbm, kv.at[0, z, 1]),
        load(2, og_hbm, og.at[n]), load(3, q_hbm, q_in), load(4, w_hbm, w),
    ]

    barrier = pltpu.get_barrier_semaphore()
    near = [at_link(step * sign) for step in (1, 2, 6, RING) for sign in (1, -1)]
    near += [at_lo(1), at_lo(2), sibling]
    for dev in near:
        pl.semaphore_signal(barrier, inc=1, device_id=dev, device_id_type=MESH)

    def greet(cond, dev, sem):
        @pl.when(cond)
        def _():
            pl.semaphore_signal(sem, inc=1, device_id=dev, device_id_type=MESH)

    for d in (1, 2, 3):
        greet(hi + d < N_HI, at_hi(d), barrier)
    wrap = (RING - 1) * LO
    greet(first, at_seq(wrap), barrier)
    greet(last, at_seq(-wrap), barrier)
    pl.semaphore_wait(barrier, len(near) + hi + jnp.where(first | last, 1, 0))
    for d in (1, 2, 3):
        greet(hi + d >= N_HI, at_hi(d), ready.at[N_HI - d])

    def way(k, r):
        return {1: 1, 2: 1, 3: 1, 4: 1 if r else -1, 5: -1, 6: -1, 7: -1, RING: RING}[k]

    def move(k, r):
        step = way(k, r)
        return copy(
            kv.at[k - step, lo_of[r]], kv.at[k, lo_of[r]], kv_send.at[k, r], kv_recv.at[k, r], at_link(step)
        )

    def wrapped():
        return copy(kv.at[RING, z], kv.at[1, z], kv_send.at[1, 0], kv_recv.at[1, 0], at_seq(-wrap))

    def shared(r):
        return copy(kv.at[RING, z], kv.at[RING, z], kv_send.at[RING, r], kv_recv.at[RING, r], at_lo(r))

    def spread(k, r):
        return copy(kv.at[k, z], kv.at[k, z], lo_send.at[k, r], lo_recv.at[k, r], at_lo(r))

    def og_copy(d):
        return copy(og.at[n], og.at[n], og_send.at[d], og_recv.at[d], at_hi(d))

    def sib_copy(d):
        m = lax.rem(hi + N_HI - d, N_HI) * 2 + core
        return copy(og.at[m], og.at[m], osib_send.at[d], osib_recv.at[d], sibling)

    loads[0].wait()
    loads[1].wait()
    go(move(RING, 0))
    go_if(not_last, move(1, 0))
    for r in (1, 2):
        go(spread(0, r))
    loads[3].wait()
    qt[...] = jnp.concatenate(
        [q_in[:, i * HD:(i + 1) * HD].astype(F32).T for i in range(GROUP)], axis=1
    ).astype(BF16)
    lane = lax.broadcasted_iota(jnp.int32, (1, WIDTH), 1)
    pos = s * TOK + lax.rem(lane, TOK)
    begin = jnp.zeros_like(pos)
    end = jnp.int32(0)
    for i in range(8):
        end = end + clip_ref[i]
        begin = jnp.where(pos >= end, end, begin)

    def part_of(k):
        at = (0, 1, 2, 3, 7, 8, 4, 5, 6)[k] * BUNDLE
        return slice(at, at + BUNDLE)

    def scores(k):
        sc = mm(kv[k, :, 0].reshape(BUNDLE, HD), qt[...])
        row = (link - k) * BUNDLE + lax.broadcasted_iota(jnp.int32, (BUNDLE, WIDTH), 0)
        ok = row >= begin
        if k == 0:
            ok = ok & (row <= pos)
        sc = jnp.where(ok, sc, MASKED)
        s_buf[k] = sc
        top = jnp.max(sc.reshape(BUNDLE // 8, 8, WIDTH), axis=0)
        mx[...] = top if k in (0, 5) else jnp.maximum(mx[...], top)
        at = part_of(k).start
        for i in range(LO):
            cols = slice(at + i * TOK, at + (i + 1) * TOK)
            kt[:, cols] = kv[k, i, 0].T
            vt[:, cols] = kv[k, i, 1].T

    def og_up(d, early):
        far = hi < 1 if d > 1 else hi > N_HI

        @pl.when((hi + d < N_HI) & (jnp.logical_not(far) if early else far))
        def _():
            pl.semaphore_wait(ready.at[d], 1)
            og_copy(d).start()

    def got(k, r, *then):
        move(k, r).wait_recv()
        for c in then:
            go(c)

    got(RING, 0, move(7, 0))
    go_if(last, wrapped())
    for r in (1, 2):
        go_if(first, shared(r))
    for r in (1, 2):
        spread(0, r).wait_recv()
        go(move(1, r))
        go_if(not_first, move(RING, r))
    loads[2].wait()
    for d in (1, 2, 3):
        go_if(hi + d >= N_HI, og_copy(d))
    go(sib_copy(0))
    got(1, 0, move(2, 0))
    got(7, 0, move(6, 0))
    scores(0)
    for r in (1, 2):
        got(RING, r, move(7, r))
        got(1, r, move(2, r))
    got(2, 0, move(3, 0))
    got(6, 0, move(5, 0))
    for d in (1, 2, 3):
        og_up(d, True)
    scores(1)
    scores(RING)
    for r in (1, 2):
        got(7, r, move(6, r))
        got(2, r, move(3, r))
    got(3, 0)
    got(5, 0, move(4, 0))
    for d in (2, 3):
        og_up(d, False)
    scores(2)
    scores(7)
    for r in (1, 2):
        got(6, r, move(5, r))
        got(3, r, move(4, r))
    scores(3)
    scores(6)
    def weigh(bundles, top):
        total = jnp.zeros((8, WIDTH), F32)
        for k in bundles:
            p = jnp.exp2(s_buf[k] * EXP2_SCALE - top)
            total = total + jnp.sum(p.reshape(BUNDLE // 8, 8, WIDTH), axis=0)
            p_buf[part_of(k), :] = p.astype(BF16)
        return jnp.sum(total, axis=0, keepdims=True)

    near_part, far_part = slice(0, 7 * BUNDLE), slice(7 * BUNDLE, 9 * BUNDLE)
    top = jnp.max(mx[...], axis=0, keepdims=True) * EXP2_SCALE
    total = weigh((0, 1, 2, 3, 6, 7, 8), top)
    near_out = mm(vt[:, near_part], p_buf[near_part, :])

    loads[4].wait()
    for d in (3, 2, 1):
        og_copy(d).wait_recv()
        go(sib_copy(d))
    for d in (0, 3, 2, 1):
        sib_copy(d).wait_recv()
    dh = mm_t(w[:, 0:WIDTH], og[0])
    for m in range(1, N_HEAD):
        dh = dh + mm_t(w[:, m * WIDTH:(m + 1) * WIDTH], og[m])
    d_t = jnp.concatenate([dh[i * HD:(i + 1) * HD, :] for i in range(GROUP)], axis=1).astype(BF16)
    dot[...] = d_t
    got(4, 0)
    for r in (1, 2):
        got(5, r)
        got(4, r)
    scores(5)
    scores(4)
    top_all = jnp.maximum(top, jnp.max(mx[...], axis=0, keepdims=True) * EXP2_SCALE)
    fade = jnp.exp2(top - top_all)
    total = total * fade + weigh((4, 5), top_all)
    inv = 1.0 / total
    out_t = near_out * fade + mm(vt[:, far_part], p_buf[far_part, :])
    out_t = (out_t * inv).astype(BF16).astype(F32)
    attended = jnp.concatenate([out_t[:, i * HD:(i + 1) * HD].T for i in range(GROUP)], axis=1).astype(BF16)
    att_ref[...] = attended

    def store(i, src, dst):
        c = pltpu.make_async_copy(src, dst, out_sem.at[i])
        c.start()
        return c

    stores = [store(0, att_ref, att_hbm)]

    def part_copy(d):
        m = lax.rem(hi + d, N_HI) * 2 + 1 - core
        return copy(part.at[m], psib.at[d], part_send.at[d], part_recv.at[d], sibling)

    def far_copy(d):
        return copy(pmine.at[d], pfar.at[d], pfar_send.at[d], pfar_recv.at[d], at_hi(d))

    for d in (1, 2, 3, 0):
        m = lax.rem(hi + d, N_HI) * 2 + 1 - core
        part[m] = mm(attended, w[:, pl.ds(pl.multiple_of(m * WIDTH, HD), WIDTH)]).astype(BF16)
        go(part_copy(d))
    for d in (1, 2, 3, 0):
        m = lax.rem(hi + d, N_HI) * 2 + core
        part[m] = mm(attended, w[:, pl.ds(pl.multiple_of(m * WIDTH, HD), WIDTH)]).astype(BF16)
    d_t = d_t.astype(F32)
    delta = jnp.sum(d_t * out_t, axis=0, keepdims=True)
    for i, factor in enumerate((inv * fade, inv)):
        dos[i] = blocks_t(d_t * factor).astype(BF16)
        qs[i] = blocks_t(qt[...].astype(F32) * (factor * SCALE)).astype(BF16)

    def backward(k):
        rows, i = part_of(k), 1 if k in (4, 5) else 0
        p = p_buf[rows, :]
        dp = mm(kv[k, :, 1].reshape(BUNDLE, HD), dot[...])
        ds = (p.astype(F32) * (dp - delta)).astype(BF16)
        dv = mm(p, dos[i])
        dk = mm(ds, qs[i])
        for i in range(LO):
            acc[k, i, 0] = dk[i * TOK:(i + 1) * TOK, :]
            acc[k, i, 1] = dv[i * TOK:(i + 1) * TOK, :]
        p_buf[rows, :] = ds

    back = [lax.rem(z + r, LO) for r in range(LO)]

    def give(k, r):
        step = way(k, r)
        return copy(stage.at[k, back[r]], come.at[k, back[r]], up_send.at[k, r], up_recv.at[k, r], at_link(-step))

    def give_wrapped():
        return copy(stage.at[1, z], come.at[1, z], up_send.at[1, 0], up_recv.at[1, 0], at_seq(wrap))

    def gather(k, r):
        return copy(stage.at[k, back[r]], mate.at[k, r], z_send.at[k, r], z_recv.at[k, r], at_lo(r))

    def fill(k, r, *terms):
        total = acc[k, back[r]]
        for t in terms:
            total = total + t.astype(F32)
        stage[k, back[r]] = total.astype(BF16)

    def send(c, k, r, *terms):
        fill(k, r, *terms)
        go(c)

    def came(k, r):
        give(k, r).wait_recv()
        return come[k, back[r]]

    def mates(k):
        for r in (1, 2):
            gather(k, r).wait_recv()
        return mate[k, 1].astype(F32) + mate[k, 2].astype(F32)

    backward(4)
    for r in (1, 2, 0):
        send(give(4, r), 4, r)
    backward(5)
    for r in (1, 2):
        send(give(5, r), 5, r)
    for d in (1, 2, 3, 0):
        part_copy(d).wait_recv()
        m = lax.rem(hi + d, N_HI) * 2 + core
        both = part[m].astype(F32) + psib[d].astype(F32)
        pmine[d] = both.astype(BF16)
        if d:
            go(far_copy(d))

    backward(3)
    backward(6)

    for r in (1, 2):
        send(give(3, r), 3, r, came(4, r))
        send(give(6, r), 6, r, came(5, r))
    send(give(3, 0), 3, 0)
    send(give(5, 0), 5, 0, came(4, 0))
    backward(7)
    backward(2)

    for r in (1, 2):
        send(give(2, r), 2, r, came(3, r))
        send(give(7, r), 7, r, came(6, r))
    send(give(2, 0), 2, 0, came(3, 0))
    send(give(6, 0), 6, 0, came(5, 0))
    backward(RING)
    backward(1)
    send(give(7, 0), 7, 0, came(6, 0))
    fill(1, 0, came(2, 0))
    go_if(not_first, give(1, 0))
    go_if(first, give_wrapped())
    for r in (1, 2):
        send(give(1, r), 1, r, came(2, r))
        fill(RING, r, came(7, r))
        go_if(not_first, give(RING, r))
        go_if(first, gather(RING, r))

    @pl.when(first)
    def _():
        fill(RING, 0, came(7, 0), mates(RING))

    @pl.when(last)
    def _():
        fill(RING, 0, came(7, 0), came(1, 0))

    @pl.when(not_first & not_last)
    def _():
        fill(RING, 0, came(7, 0))

    go(give(RING, 0))
    backward(0)
    for r in (1, 2):

        @pl.when(first)
        def _():
            fill(0, r, came(1, r))

        @pl.when(not_first)
        def _():
            fill(0, r, came(1, r), came(RING, r))

        go(gather(0, r))

    dq_t = mm(kt[:, near_part], p_buf[near_part, :]) * fade + mm(kt[:, far_part], p_buf[far_part, :])
    dq_t = dq_t * (inv * SCALE)
    dq_ref[...] = jnp.concatenate([dq_t[:, i * HD:(i + 1) * HD].T for i in range(GROUP)], axis=1).astype(BF16)
    stores.append(store(1, dq_ref, dq_hbm))

    for d in (1, 2, 3):
        far_copy(d).wait_recv()
    mixed_ref[...] = (
        pmine[0].astype(F32) + pfar[1].astype(F32) + pfar[2].astype(F32) + pfar[3].astype(F32)
    ).astype(BF16)
    stores.append(store(2, mixed_ref, mixed_hbm))

    @pl.when(not_last)
    def _():
        acc[0, z] = acc[0, z] + came(1, 0).astype(F32)

    own = acc[0, z]
    own = own + came(RING, 0).astype(F32)
    own = own + mates(0)
    dk_ref[...] = own[0].astype(BF16)
    dv_ref[...] = own[1].astype(BF16)
    stores.append(store(3, dk_ref, dk_hbm))
    stores.append(store(4, dv_ref, dv_hbm))

    for d in (1, 2, 3):
        sent.append((hi + d < N_HI, og_copy(d)))
    for cond, c in sent:
        c.wait_send() if cond is None else pl.when(cond)(c.wait_send)
    for c in stores:
        c.wait()


def finish(*refs):
    for source, target in zip(refs[:5], refs[5:]):
        target[...] = source[...]


def shards(query_heads, key_heads, value_heads, out_weight, out_grad, clip_lengths):
    dma = pltpu.SemaphoreType.DMA
    vmem = pltpu.VMEM
    keys = (RING + 1) * BUNDLE
    hbm = pl.BlockSpec(memory_space=pl.ANY)
    block = jax.ShapeDtypeStruct((TOK, WIDTH), BF16)
    small = jax.ShapeDtypeStruct((TOK, HD), BF16)
    shapes = (block, block, block, small, small)
    piece = (2, TOK, HD)
    results = pl.pallas_call(
        kernel,
        out_shape=shapes,
        in_specs=[pl.BlockSpec(memory_space=pltpu.SMEM)] + [hbm] * 5,
        out_specs=[hbm] * 5,
        scratch_shapes=[
            vmem((TOK, WIDTH), BF16),
            vmem((RING + 1, LO) + piece, BF16),
            vmem((N_HEAD, TOK, WIDTH), BF16),
            vmem((WIDTH, N_HEAD * WIDTH), BF16),
            vmem((HD, WIDTH), BF16),
            vmem((2, WIDTH, HD), BF16),
            vmem((HD, WIDTH), BF16),
            vmem((2, WIDTH, HD), BF16),
            vmem((RING + 1, BUNDLE, WIDTH), F32),
            vmem((keys, WIDTH), BF16),
            vmem((HD, keys), BF16),
            vmem((HD, keys), BF16),
            vmem((8, WIDTH), F32),
            vmem((RING + 1, LO) + piece, F32),
            vmem((N_HEAD, TOK, WIDTH), BF16),
            vmem((N_HI, TOK, WIDTH), BF16),
            vmem((N_HI, TOK, WIDTH), BF16),
            vmem((N_HI, TOK, WIDTH), BF16),
            vmem((RING + 1, LO) + piece, BF16),
            vmem((RING + 1, LO) + piece, BF16),
            vmem((RING + 1, LO) + piece, BF16),
            vmem((TOK, WIDTH), BF16), vmem((TOK, WIDTH), BF16), vmem((TOK, WIDTH), BF16),
            vmem((TOK, HD), BF16), vmem((TOK, HD), BF16),
            dma((5,)), dma((5,)), pltpu.SemaphoreType.REGULAR((N_HI,)),
            dma((RING + 1, LO)), dma((RING + 1, LO)), dma((RING + 1, LO)), dma((RING + 1, LO)),
            dma((N_HI,)), dma((N_HI,)), dma((N_HI,)), dma((N_HI,)),
            dma((N_HI,)), dma((N_HI,)), dma((N_HI,)), dma((N_HI,)),
            dma((RING + 1, LO)), dma((RING + 1, LO)), dma((RING + 1, LO)), dma((RING + 1, LO)),
        ],
        compiler_params=pltpu.CompilerParams(
            collective_id=0, has_side_effects=True, vmem_limit_bytes=60 * 1024 * 1024
        ),
        cost_estimate=pl.CostEstimate(flops=3_000_000_000, bytes_accessed=4_000_000, transcendentals=1_400_000),
    )(clip_lengths, query_heads, key_heads, value_heads, out_grad, out_weight)
    return pl.pallas_call(
        finish,
        out_shape=shapes,
        in_specs=[pl.BlockSpec(memory_space=pltpu.VMEM)] * 5,
        out_specs=[pl.BlockSpec(memory_space=pltpu.VMEM)] * 5,
        compiler_params=pltpu.CompilerParams(vmem_limit_bytes=60 * 1024 * 1024),
    )(*results)


def solution(mesh):
    wide = P("seq", "head")
    return jax.shard_map(
        shards,
        mesh=mesh,
        in_specs=(wide, wide, wide, P("head", None), wide, P()),
        out_specs=(wide,) * 5,
        check_vma=False,
    )
```

```python
import math

import jax
import jax.numpy as jnp
from jax import lax
from jax.experimental import pallas as pl
from jax.experimental.pallas import tpu as pltpu
from jax.sharding import PartitionSpec as P

HD = 128
GROUP = 3
TOK = 128
LO = 3
LINKS = 32
RING = 8
N_SEQ = LO * LINKS
N_HEAD = 8
N_HI = 4
WIDTH = GROUP * HD
BUNDLE = LO * TOK
SCALE = 1.0 / math.sqrt(HD)
EXP2_SCALE = SCALE * math.log2(math.e)
MASKED = -1e30
MESH = pl.DeviceIdType.MESH
F32 = jnp.float32
BF16 = jnp.bfloat16


def mm(a, b):
    return jnp.dot(a, b, preferred_element_type=F32)


def mm_t(a, b):
    return lax.dot_general(a, b, (((1,), (1,)), ((), ())), preferred_element_type=F32)


def blocks_t(x):
    if x.shape[0] == HD:
        return jnp.concatenate([x[:, i * HD:(i + 1) * HD].T for i in range(GROUP)], axis=0)
    return jnp.concatenate([x[i * HD:(i + 1) * HD, :].T for i in range(GROUP)], axis=1)


def kernel(
    clip_ref, q_hbm, k_hbm, v_hbm, og_hbm, w_hbm,
    mixed_hbm, att_hbm, dq_hbm, dk_hbm, dv_hbm,
    q_in, kv, og, w, qt, qs, dot, dos, s_buf, p_buf, kt, vt, mx, acc,
    part, psib, pmine, pfar, come, mate, stage,
    mixed_ref, att_ref, dq_ref, dk_ref, dv_ref,
    in_sem, out_sem, ready,
    kv_send, kv_recv, lo_send, lo_recv, og_send, og_recv, osib_send, osib_recv,
    part_send, part_recv, pfar_send, pfar_recv,
    up_send, up_recv, z_send, z_recv,
):
    s = lax.axis_index("seq")
    n = lax.axis_index("head")
    link, z = lax.div(s, LO), lax.rem(s, LO)
    hi, core = lax.div(n, 2), lax.rem(n, 2)
    y = lax.rem(link, RING)
    first, last = y == 0, y == RING - 1
    not_first, not_last = y > 0, y < RING - 1

    def at_seq(step):
        return (lax.rem(s + step + N_SEQ, N_SEQ), n)

    def at_link(step):
        return at_seq(step * LO)

    def at_lo(r):
        return (link * LO + lax.rem(z + r, LO), n)

    def at_hi(d):
        return (s, lax.rem(hi + d, N_HI) * 2 + core)

    sibling = (s, hi * 2 + 1 - core)
    lo_of = [lax.rem(z + LO - r, LO) for r in range(LO)]

    def copy(src, dst, ssem, rsem, dev):
        return pltpu.make_async_remote_copy(
            src_ref=src, dst_ref=dst, send_sem=ssem, recv_sem=rsem, device_id=dev, device_id_type=MESH
        )

    sent = []

    def go(c):
        c.start()
        sent.append((None, c))

    def go_if(cond, c):
        pl.when(cond)(c.start)
        sent.append((cond, c))

    def load(i, src, dst):
        c = pltpu.make_async_copy(src, dst, in_sem.at[i])
        c.start()
        return c

    loads = [
        load(0, k_hbm, kv.at[0, z, 0]), load(1, v_hbm, kv.at[0, z, 1]),
        load(2, og_hbm, og.at[n]), load(3, q_hbm, q_in), load(4, w_hbm, w),
    ]

    barrier = pltpu.get_barrier_semaphore()
    near = [at_link(step * sign) for step in (1, 2, 6, RING) for sign in (1, -1)]
    near += [at_lo(1), at_lo(2), sibling]
    for dev in near:
        pl.semaphore_signal(barrier, inc=1, device_id=dev, device_id_type=MESH)

    def greet(cond, dev, sem):
        @pl.when(cond)
        def _():
            pl.semaphore_signal(sem, inc=1, device_id=dev, device_id_type=MESH)

    for d in (1, 2, 3):
        greet(hi + d < N_HI, at_hi(d), barrier)
    wrap = (RING - 1) * LO
    greet(first, at_seq(wrap), barrier)
    greet(last, at_seq(-wrap), barrier)
    pl.semaphore_wait(barrier, len(near) + hi + jnp.where(first | last, 1, 0))
    for d in (1, 2, 3):
        greet(hi + d >= N_HI, at_hi(d), ready.at[N_HI - d])

    def way(k, r):
        return {1: 1, 2: 1, 3: 1, 4: 1 if r else -1, 5: -1, 6: -1, 7: -1, RING: RING}[k]

    def move(k, r):
        step = way(k, r)
        return copy(
            kv.at[k - step, lo_of[r]], kv.at[k, lo_of[r]], kv_send.at[k, r], kv_recv.at[k, r], at_link(step)
        )

    def wrapped():
        return copy(kv.at[RING, z], kv.at[1, z], kv_send.at[1, 0], kv_recv.at[1, 0], at_seq(-wrap))

    def shared(r):
        return copy(kv.at[RING, z], kv.at[RING, z], kv_send.at[RING, r], kv_recv.at[RING, r], at_lo(r))

    def spread(k, r):
        return copy(kv.at[k, z], kv.at[k, z], lo_send.at[k, r], lo_recv.at[k, r], at_lo(r))

    def og_copy(d):
        return copy(og.at[n], og.at[n], og_send.at[d], og_recv.at[d], at_hi(d))

    def sib_copy(d):
        m = lax.rem(hi + N_HI - d, N_HI) * 2 + core
        return copy(og.at[m], og.at[m], osib_send.at[d], osib_recv.at[d], sibling)

    loads[0].wait()
    loads[1].wait()
    go(move(RING, 0))
    go_if(not_last, move(1, 0))
    for r in (1, 2):
        go(spread(0, r))
    loads[3].wait()
    qt[...] = jnp.concatenate(
        [q_in[:, i * HD:(i + 1) * HD].astype(F32).T for i in range(GROUP)], axis=1
    ).astype(BF16)
    lane = lax.broadcasted_iota(jnp.int32, (1, WIDTH), 1)
    pos = s * TOK + lax.rem(lane, TOK)
    begin = jnp.zeros_like(pos)
    end = jnp.int32(0)
    for i in range(8):
        end = end + clip_ref[i]
        begin = jnp.where(pos >= end, end, begin)

    def part_of(k):
        at = (0, 1, 2, 3, 7, 8, 4, 5, 6)[k] * BUNDLE
        return slice(at, at + BUNDLE)

    def scores(k):
        sc = mm(kv[k, :, 0].reshape(BUNDLE, HD), qt[...])
        row = (link - k) * BUNDLE + lax.broadcasted_iota(jnp.int32, (BUNDLE, WIDTH), 0)
        ok = row >= begin
        if k == 0:
            ok = ok & (row <= pos)
        sc = jnp.where(ok, sc, MASKED)
        s_buf[k] = sc
        top = jnp.max(sc.reshape(BUNDLE // 8, 8, WIDTH), axis=0)
        mx[...] = top if k in (0, 5) else jnp.maximum(mx[...], top)
        at = part_of(k).start
        for i in range(LO):
            cols = slice(at + i * TOK, at + (i + 1) * TOK)
            vt[:, cols] = kv[k, i, 1].T

    def og_up(d, early):
        far = hi < 1 if d > 1 else hi > N_HI

        @pl.when((hi + d < N_HI) & (jnp.logical_not(far) if early else far))
        def _():
            pl.semaphore_wait(ready.at[d], 1)
            og_copy(d).start()

    def got(k, r, *then):
        move(k, r).wait_recv()
        for c in then:
            go(c)

    got(RING, 0, move(7, 0))
    go_if(last, wrapped())
    for r in (1, 2):
        go_if(first, shared(r))
    for r in (1, 2):
        spread(0, r).wait_recv()
        go(move(1, r))
        go_if(not_first, move(RING, r))
    loads[2].wait()
    for d in (1, 2, 3):
        go_if(hi + d >= N_HI, og_copy(d))
    go(sib_copy(0))
    got(1, 0, move(2, 0))
    got(7, 0, move(6, 0))
    scores(0)
    for r in (1, 2):
        got(RING, r, move(7, r))
        got(1, r, move(2, r))
    got(2, 0, move(3, 0))
    got(6, 0, move(5, 0))
    for d in (1, 2, 3):
        og_up(d, True)
    scores(1)
    scores(RING)
    for r in (1, 2):
        got(7, r, move(6, r))
        got(2, r, move(3, r))
    got(3, 0)
    got(5, 0, move(4, 0))
    for d in (2, 3):
        og_up(d, False)
    scores(2)
    scores(7)
    for r in (1, 2):
        got(6, r, move(5, r))
        got(3, r, move(4, r))
    scores(3)
    scores(6)
    def weigh(bundles, top):
        total = jnp.zeros((8, WIDTH), F32)
        for k in bundles:
            p = jnp.exp2(s_buf[k] * EXP2_SCALE - top)
            total = total + jnp.sum(p.reshape(BUNDLE // 8, 8, WIDTH), axis=0)
            p_buf[part_of(k), :] = p.astype(BF16)
        return jnp.sum(total, axis=0, keepdims=True)

    near_part, far_part = slice(0, 7 * BUNDLE), slice(7 * BUNDLE, 9 * BUNDLE)
    top = jnp.max(mx[...], axis=0, keepdims=True) * EXP2_SCALE
    total = weigh((0, 1, 2, 3, 6, 7, 8), top)
    near_out = mm(vt[:, near_part], p_buf[near_part, :])

    loads[4].wait()
    for d in (3, 2, 1):
        og_copy(d).wait_recv()
        go(sib_copy(d))
    for d in (0, 3, 2, 1):
        sib_copy(d).wait_recv()
    dh = mm_t(w[:, 0:WIDTH], og[0])
    for m in range(1, N_HEAD):
        dh = dh + mm_t(w[:, m * WIDTH:(m + 1) * WIDTH], og[m])
    d_t = jnp.concatenate([dh[i * HD:(i + 1) * HD, :] for i in range(GROUP)], axis=1).astype(BF16)
    dot[...] = d_t
    got(4, 0)
    for r in (1, 2):
        got(5, r)
        got(4, r)
    scores(5)
    scores(4)
    top_all = jnp.maximum(top, jnp.max(mx[...], axis=0, keepdims=True) * EXP2_SCALE)
    fade = jnp.exp2(top - top_all)
    total = total * fade + weigh((4, 5), top_all)
    inv = 1.0 / total
    out_t = near_out * fade + mm(vt[:, far_part], p_buf[far_part, :])
    out_t = (out_t * inv).astype(BF16).astype(F32)
    attended = jnp.concatenate([out_t[:, i * HD:(i + 1) * HD].T for i in range(GROUP)], axis=1).astype(BF16)
    att_ref[...] = attended

    def store(i, src, dst):
        c = pltpu.make_async_copy(src, dst, out_sem.at[i])
        c.start()
        return c

    stores = [store(0, att_ref, att_hbm)]

    def part_copy(d):
        m = lax.rem(hi + d, N_HI) * 2 + 1 - core
        return copy(part.at[m], psib.at[d], part_send.at[d], part_recv.at[d], sibling)

    def far_copy(d):
        return copy(pmine.at[d], pfar.at[d], pfar_send.at[d], pfar_recv.at[d], at_hi(d))

    for d in (1, 2, 3, 0):
        m = lax.rem(hi + d, N_HI) * 2 + 1 - core
        part[m] = mm(attended, w[:, pl.ds(pl.multiple_of(m * WIDTH, HD), WIDTH)]).astype(BF16)
        go(part_copy(d))
    d_t = d_t.astype(F32)
    delta = jnp.sum(d_t * out_t, axis=0, keepdims=True)
    for i, factor in enumerate((inv * fade, inv)):
        dos[i] = blocks_t(d_t * factor).astype(BF16)
        qs[i] = blocks_t(qt[...].astype(F32) * (factor * SCALE)).astype(BF16)

    def backward(k):
        rows, i = part_of(k), 1 if k in (4, 5) else 0
        p = p_buf[rows, :]
        dp = mm(kv[k, :, 1].reshape(BUNDLE, HD), dot[...])
        ds = (p.astype(F32) * (dp - delta)).astype(BF16)
        dv = mm(p, dos[i])
        dk = mm(ds, qs[i])
        for i in range(LO):
            acc[k, i, 0] = dk[i * TOK:(i + 1) * TOK, :]
            acc[k, i, 1] = dv[i * TOK:(i + 1) * TOK, :]
            kt[:, rows.start + i * TOK:rows.start + (i + 1) * TOK] = kv[k, i, 0].T
        p_buf[rows, :] = ds

    back = [lax.rem(z + r, LO) for r in range(LO)]

    def give(k, r):
        step = way(k, r)
        return copy(stage.at[k, back[r]], come.at[k, back[r]], up_send.at[k, r], up_recv.at[k, r], at_link(-step))

    def give_wrapped():
        return copy(stage.at[1, z], come.at[1, z], up_send.at[1, 0], up_recv.at[1, 0], at_seq(wrap))

    def gather(k, r):
        return copy(stage.at[k, back[r]], mate.at[k, r], z_send.at[k, r], z_recv.at[k, r], at_lo(r))

    def fill(k, r, *terms):
        total = acc[k, back[r]]
        for t in terms:
            total = total + t.astype(F32)
        stage[k, back[r]] = total.astype(BF16)

    def send(c, k, r, *terms):
        fill(k, r, *terms)
        go(c)

    def came(k, r):
        give(k, r).wait_recv()
        return come[k, back[r]]

    def mates(k):
        for r in (1, 2):
            gather(k, r).wait_recv()
        return mate[k, 1].astype(F32) + mate[k, 2].astype(F32)

    backward(4)
    for r in (1, 2, 0):
        send(give(4, r), 4, r)
    backward(5)
    for r in (1, 2):
        send(give(5, r), 5, r)
    for d in (1, 2, 3, 0):
        m = lax.rem(hi + d, N_HI) * 2 + core
        part[m] = mm(attended, w[:, pl.ds(pl.multiple_of(m * WIDTH, HD), WIDTH)]).astype(BF16)
    for d in (1, 2, 3, 0):
        part_copy(d).wait_recv()
        m = lax.rem(hi + d, N_HI) * 2 + core
        both = part[m].astype(F32) + psib[d].astype(F32)
        pmine[d] = both.astype(BF16)
        if d:
            go(far_copy(d))

    backward(3)
    backward(6)

    for r in (1, 2):
        send(give(3, r), 3, r, came(4, r))
        send(give(6, r), 6, r, came(5, r))
    send(give(3, 0), 3, 0)
    send(give(5, 0), 5, 0, came(4, 0))
    backward(7)
    backward(2)

    for r in (1, 2):
        send(give(2, r), 2, r, came(3, r))
        send(give(7, r), 7, r, came(6, r))
    send(give(2, 0), 2, 0, came(3, 0))
    send(give(6, 0), 6, 0, came(5, 0))
    backward(RING)
    backward(1)
    for r in (1, 2):
        send(give(1, r), 1, r, came(2, r))
        fill(RING, r, came(7, r))
        go_if(not_first, give(RING, r))
        go_if(first, gather(RING, r))
    send(give(7, 0), 7, 0, came(6, 0))
    fill(1, 0, came(2, 0))
    go_if(not_first, give(1, 0))
    go_if(first, give_wrapped())

    @pl.when(first)
    def _():
        fill(RING, 0, came(7, 0), mates(RING))

    @pl.when(last)
    def _():
        fill(RING, 0, came(7, 0), came(1, 0))

    @pl.when(not_first & not_last)
    def _():
        fill(RING, 0, came(7, 0))

    go(give(RING, 0))
    backward(0)
    for r in (1, 2):

        @pl.when(first)
        def _():
            fill(0, r, came(1, r))

        @pl.when(not_first)
        def _():
            fill(0, r, came(1, r), came(RING, r))

        go(gather(0, r))

    dq_t = mm(kt[:, near_part], p_buf[near_part, :]) * fade + mm(kt[:, far_part], p_buf[far_part, :])
    dq_t = dq_t * (inv * SCALE)
    dq_ref[...] = jnp.concatenate([dq_t[:, i * HD:(i + 1) * HD].T for i in range(GROUP)], axis=1).astype(BF16)
    stores.append(store(1, dq_ref, dq_hbm))

    for d in (1, 2, 3):
        far_copy(d).wait_recv()
    mixed_ref[...] = (
        pmine[0].astype(F32) + pfar[1].astype(F32) + pfar[2].astype(F32) + pfar[3].astype(F32)
    ).astype(BF16)
    stores.append(store(2, mixed_ref, mixed_hbm))

    @pl.when(not_last)
    def _():
        acc[0, z] = acc[0, z] + came(1, 0).astype(F32)

    own = acc[0, z]
    own = own + came(RING, 0).astype(F32)
    own = own + mates(0)
    dk_ref[...] = own[0].astype(BF16)
    dv_ref[...] = own[1].astype(BF16)
    stores.append(store(3, dk_ref, dk_hbm))
    stores.append(store(4, dv_ref, dv_hbm))

    for d in (1, 2, 3):
        sent.append((hi + d < N_HI, og_copy(d)))
    for cond, c in sent:
        c.wait_send() if cond is None else pl.when(cond)(c.wait_send)
    for c in stores:
        c.wait()


def finish(*refs):
    for source, target in zip(refs[:5], refs[5:]):
        target[...] = source[...]


def shards(query_heads, key_heads, value_heads, out_weight, out_grad, clip_lengths):
    dma = pltpu.SemaphoreType.DMA
    vmem = pltpu.VMEM
    keys = (RING + 1) * BUNDLE
    hbm = pl.BlockSpec(memory_space=pl.ANY)
    block = jax.ShapeDtypeStruct((TOK, WIDTH), BF16)
    small = jax.ShapeDtypeStruct((TOK, HD), BF16)
    shapes = (block, block, block, small, small)
    piece = (2, TOK, HD)
    results = pl.pallas_call(
        kernel,
        out_shape=shapes,
        in_specs=[pl.BlockSpec(memory_space=pltpu.SMEM)] + [hbm] * 5,
        out_specs=[hbm] * 5,
        scratch_shapes=[
            vmem((TOK, WIDTH), BF16),
            vmem((RING + 1, LO) + piece, BF16),
            vmem((N_HEAD, TOK, WIDTH), BF16),
            vmem((WIDTH, N_HEAD * WIDTH), BF16),
            vmem((HD, WIDTH), BF16),
            vmem((2, WIDTH, HD), BF16),
            vmem((HD, WIDTH), BF16),
            vmem((2, WIDTH, HD), BF16),
            vmem((RING + 1, BUNDLE, WIDTH), F32),
            vmem((keys, WIDTH), BF16),
            vmem((HD, keys), BF16),
            vmem((HD, keys), BF16),
            vmem((8, WIDTH), F32),
            vmem((RING + 1, LO) + piece, F32),
            vmem((N_HEAD, TOK, WIDTH), BF16),
            vmem((N_HI, TOK, WIDTH), BF16),
            vmem((N_HI, TOK, WIDTH), BF16),
            vmem((N_HI, TOK, WIDTH), BF16),
            vmem((RING + 1, LO) + piece, BF16),
            vmem((RING + 1, LO) + piece, BF16),
            vmem((RING + 1, LO) + piece, BF16),
            vmem((TOK, WIDTH), BF16), vmem((TOK, WIDTH), BF16), vmem((TOK, WIDTH), BF16),
            vmem((TOK, HD), BF16), vmem((TOK, HD), BF16),
            dma((5,)), dma((5,)), pltpu.SemaphoreType.REGULAR((N_HI,)),
            dma((RING + 1, LO)), dma((RING + 1, LO)), dma((RING + 1, LO)), dma((RING + 1, LO)),
            dma((N_HI,)), dma((N_HI,)), dma((N_HI,)), dma((N_HI,)),
            dma((N_HI,)), dma((N_HI,)), dma((N_HI,)), dma((N_HI,)),
            dma((RING + 1, LO)), dma((RING + 1, LO)), dma((RING + 1, LO)), dma((RING + 1, LO)),
        ],
        compiler_params=pltpu.CompilerParams(
            collective_id=0, has_side_effects=True, vmem_limit_bytes=60 * 1024 * 1024
        ),
        cost_estimate=pl.CostEstimate(flops=3_000_000_000, bytes_accessed=4_000_000, transcendentals=1_400_000),
    )(clip_lengths, query_heads, key_heads, value_heads, out_grad, out_weight)
    return pl.pallas_call(
        finish,
        out_shape=shapes,
        in_specs=[pl.BlockSpec(memory_space=pltpu.VMEM)] * 5,
        out_specs=[pl.BlockSpec(memory_space=pltpu.VMEM)] * 5,
        compiler_params=pltpu.CompilerParams(vmem_limit_bytes=60 * 1024 * 1024),
    )(*results)


def solution(mesh):
    wide = P("seq", "head")
    return jax.shard_map(
        shards,
        mesh=mesh,
        in_specs=(wide, wide, wide, P("head", None), wide, P()),
        out_specs=(wide,) * 5,
        check_vma=False,
    )
```

```python
import math

import jax
import jax.numpy as jnp
from jax import lax
from jax.experimental import pallas as pl
from jax.experimental.pallas import tpu as pltpu
from jax.sharding import PartitionSpec as P

HD = 128
GROUP = 3
TOK = 128
LO = 3
LINKS = 32
RING = 8
N_SEQ = LO * LINKS
N_HEAD = 8
N_HI = 4
WIDTH = GROUP * HD
BUNDLE = LO * TOK
SCALE = 1.0 / math.sqrt(HD)
EXP2_SCALE = SCALE * math.log2(math.e)
MASKED = -1e30
MESH = pl.DeviceIdType.MESH
F32 = jnp.float32
BF16 = jnp.bfloat16


def mm(a, b):
    return jnp.dot(a, b, preferred_element_type=F32)


def mm_t(a, b):
    return lax.dot_general(a, b, (((1,), (1,)), ((), ())), preferred_element_type=F32)


def blocks_t(x):
    if x.shape[0] == HD:
        return jnp.concatenate([x[:, i * HD:(i + 1) * HD].T for i in range(GROUP)], axis=0)
    return jnp.concatenate([x[i * HD:(i + 1) * HD, :].T for i in range(GROUP)], axis=1)


def kernel(
    clip_ref, q_hbm, k_hbm, v_hbm, og_hbm, w_hbm,
    mixed_hbm, att_hbm, dq_hbm, dk_hbm, dv_hbm,
    q_in, kv, og, w, qt, qs, dot, dos, s_buf, p_buf, kt, vt, mx, acc,
    part, psib, pmine, pfar, come, mate, stage,
    mixed_ref, att_ref, dq_ref, dk_ref, dv_ref,
    in_sem, out_sem, ready,
    kv_send, kv_recv, lo_send, lo_recv, og_send, og_recv, osib_send, osib_recv,
    part_send, part_recv, pfar_send, pfar_recv,
    up_send, up_recv, z_send, z_recv,
):
    s = lax.axis_index("seq")
    n = lax.axis_index("head")
    link, z = lax.div(s, LO), lax.rem(s, LO)
    hi, core = lax.div(n, 2), lax.rem(n, 2)
    y = lax.rem(link, RING)
    first, last = y == 0, y == RING - 1
    not_first, not_last = y > 0, y < RING - 1

    def at_seq(step):
        return (lax.rem(s + step + N_SEQ, N_SEQ), n)

    def at_link(step):
        return at_seq(step * LO)

    def at_lo(r):
        return (link * LO + lax.rem(z + r, LO), n)

    def at_hi(d):
        return (s, lax.rem(hi + d, N_HI) * 2 + core)

    sibling = (s, hi * 2 + 1 - core)
    lo_of = [lax.rem(z + LO - r, LO) for r in range(LO)]

    def copy(src, dst, ssem, rsem, dev):
        return pltpu.make_async_remote_copy(
            src_ref=src, dst_ref=dst, send_sem=ssem, recv_sem=rsem, device_id=dev, device_id_type=MESH
        )

    sent = []

    def go(c):
        c.start()
        sent.append((None, c))

    def go_if(cond, c):
        pl.when(cond)(c.start)
        sent.append((cond, c))

    def load(i, src, dst):
        c = pltpu.make_async_copy(src, dst, in_sem.at[i])
        c.start()
        return c

    loads = [
        load(0, k_hbm, kv.at[0, z, 0]), load(1, v_hbm, kv.at[0, z, 1]),
        load(2, og_hbm, og.at[n]), load(3, q_hbm, q_in), load(4, w_hbm, w),
    ]

    barrier = pltpu.get_barrier_semaphore()
    near = [at_link(step * sign) for step in (1, 2, 6, RING) for sign in (1, -1)]
    near += [at_lo(1), at_lo(2), sibling]
    for dev in near:
        pl.semaphore_signal(barrier, inc=1, device_id=dev, device_id_type=MESH)

    def greet(cond, dev, sem):
        @pl.when(cond)
        def _():
            pl.semaphore_signal(sem, inc=1, device_id=dev, device_id_type=MESH)

    for d in (1, 2, 3):
        greet(hi + d < N_HI, at_hi(d), barrier)
    wrap = (RING - 1) * LO
    greet(first, at_seq(wrap), barrier)
    greet(last, at_seq(-wrap), barrier)
    pl.semaphore_wait(barrier, len(near) + hi + jnp.where(first | last, 1, 0))
    for d in (1, 2, 3):
        greet(hi + d >= N_HI, at_hi(d), ready.at[N_HI - d])

    def way(k, r):
        return {1: 1, 2: 1, 3: 1, 4: 1 if r else -1, 5: -1, 6: -1, 7: -1, RING: RING}[k]

    def move(k, r):
        step = way(k, r)
        return copy(
            kv.at[k - step, lo_of[r]], kv.at[k, lo_of[r]], kv_send.at[k, r], kv_recv.at[k, r], at_link(step)
        )

    def wrapped():
        return copy(kv.at[RING, z], kv.at[1, z], kv_send.at[1, 0], kv_recv.at[1, 0], at_seq(-wrap))

    def shared(r):
        return copy(kv.at[RING, z], kv.at[RING, z], kv_send.at[RING, r], kv_recv.at[RING, r], at_lo(r))

    def spread(k, r):
        return copy(kv.at[k, z], kv.at[k, z], lo_send.at[k, r], lo_recv.at[k, r], at_lo(r))

    def og_copy(d):
        return copy(og.at[n], og.at[n], og_send.at[d], og_recv.at[d], at_hi(d))

    def sib_copy(d):
        m = lax.rem(hi + N_HI - d, N_HI) * 2 + core
        return copy(og.at[m], og.at[m], osib_send.at[d], osib_recv.at[d], sibling)

    loads[0].wait()
    loads[1].wait()
    go(move(RING, 0))
    go_if(not_last, move(1, 0))
    for r in (1, 2):
        go(spread(0, r))
    loads[3].wait()
    qt[...] = jnp.concatenate(
        [q_in[:, i * HD:(i + 1) * HD].astype(F32).T for i in range(GROUP)], axis=1
    ).astype(BF16)
    lane = lax.broadcasted_iota(jnp.int32, (1, WIDTH), 1)
    pos = s * TOK + lax.rem(lane, TOK)
    begin = jnp.zeros_like(pos)
    end = jnp.int32(0)
    for i in range(8):
        end = end + clip_ref[i]
        begin = jnp.where(pos >= end, end, begin)

    def part_of(k):
        at = (0, 1, 2, 3, 7, 8, 4, 5, 6)[k] * BUNDLE
        return slice(at, at + BUNDLE)

    def scores(k):
        sc = mm(kv[k, :, 0].reshape(BUNDLE, HD), qt[...])
        row = (link - k) * BUNDLE + lax.broadcasted_iota(jnp.int32, (BUNDLE, WIDTH), 0)
        ok = row >= begin
        if k == 0:
            ok = ok & (row <= pos)
        sc = jnp.where(ok, sc, MASKED)
        s_buf[k] = sc
        top = jnp.max(sc.reshape(BUNDLE // 8, 8, WIDTH), axis=0)
        mx[...] = top if k in (0, 5) else jnp.maximum(mx[...], top)
        at = part_of(k).start
        for i in range(LO):
            cols = slice(at + i * TOK, at + (i + 1) * TOK)
            vt[:, cols] = kv[k, i, 1].T

    def og_up(d, early):
        far = hi < 1 if d > 1 else hi > N_HI

        @pl.when((hi + d < N_HI) & (jnp.logical_not(far) if early else far))
        def _():
            pl.semaphore_wait(ready.at[d], 1)
            og_copy(d).start()

    def got(k, r, *then):
        move(k, r).wait_recv()
        for c in then:
            go(c)

    got(RING, 0, move(7, 0))
    go_if(last, wrapped())
    for r in (1, 2):
        go_if(first, shared(r))
    for r in (1, 2):
        spread(0, r).wait_recv()
        go(move(1, r))
        go_if(not_first, move(RING, r))
    loads[2].wait()
    for d in (1, 2, 3):
        go_if(hi + d >= N_HI, og_copy(d))
    go(sib_copy(0))
    got(1, 0, move(2, 0))
    got(7, 0, move(6, 0))
    scores(0)
    for r in (1, 2):
        got(RING, r, move(7, r))
        got(1, r, move(2, r))
    got(2, 0, move(3, 0))
    got(6, 0, move(5, 0))
    for d in (1, 2, 3):
        og_up(d, True)
    scores(1)
    scores(RING)
    for r in (1, 2):
        got(7, r, move(6, r))
        got(2, r, move(3, r))
    got(3, 0)
    got(5, 0, move(4, 0))
    for d in (2, 3):
        og_up(d, False)
    scores(2)
    scores(7)
    for r in (1, 2):
        got(6, r, move(5, r))
        got(3, r, move(4, r))
    scores(3)
    scores(6)
    def weigh(bundles, top):
        total = jnp.zeros((8, WIDTH), F32)
        for k in bundles:
            p = jnp.exp2(s_buf[k] * EXP2_SCALE - top)
            total = total + jnp.sum(p.reshape(BUNDLE // 8, 8, WIDTH), axis=0)
            p_buf[part_of(k), :] = p.astype(BF16)
        return jnp.sum(total, axis=0, keepdims=True)

    near_part, far_part = slice(0, 7 * BUNDLE), slice(7 * BUNDLE, 9 * BUNDLE)
    top = jnp.max(mx[...], axis=0, keepdims=True) * EXP2_SCALE
    total = weigh((0, 1, 2, 3, 6, 7, 8), top)
    near_out = mm(vt[:, near_part], p_buf[near_part, :])

    loads[4].wait()
    for d in (3, 2, 1):
        og_copy(d).wait_recv()
        go(sib_copy(d))
    for d in (0, 3, 2, 1):
        sib_copy(d).wait_recv()
    dh = mm_t(w[:, 0:WIDTH], og[0])
    for m in range(1, N_HEAD):
        dh = dh + mm_t(w[:, m * WIDTH:(m + 1) * WIDTH], og[m])
    d_t = jnp.concatenate([dh[i * HD:(i + 1) * HD, :] for i in range(GROUP)], axis=1).astype(BF16)
    dot[...] = d_t
    got(4, 0)
    for r in (1, 2):
        got(5, r)
        got(4, r)
    scores(5)
    scores(4)
    top_all = jnp.maximum(top, jnp.max(mx[...], axis=0, keepdims=True) * EXP2_SCALE)
    fade = jnp.exp2(top - top_all)
    total = total * fade + weigh((4, 5), top_all)
    inv = 1.0 / total
    out_t = near_out * fade + mm(vt[:, far_part], p_buf[far_part, :])
    out_t = (out_t * inv).astype(BF16).astype(F32)
    d_t = d_t.astype(F32)
    delta = jnp.sum(d_t * out_t, axis=0, keepdims=True)

    def scale_rows(i, factor):
        dos[i] = blocks_t(d_t * factor).astype(BF16)
        qs[i] = blocks_t(qt[...].astype(F32) * (factor * SCALE)).astype(BF16)

    scale_rows(1, inv)

    def backward(k):
        rows, i = part_of(k), 1 if k in (4, 5) else 0
        p = p_buf[rows, :]
        dp = mm(kv[k, :, 1].reshape(BUNDLE, HD), dot[...])
        ds = (p.astype(F32) * (dp - delta)).astype(BF16)
        dv = mm(p, dos[i])
        dk = mm(ds, qs[i])
        for i in range(LO):
            acc[k, i, 0] = dk[i * TOK:(i + 1) * TOK, :]
            acc[k, i, 1] = dv[i * TOK:(i + 1) * TOK, :]
            kt[:, rows.start + i * TOK:rows.start + (i + 1) * TOK] = kv[k, i, 0].T
        p_buf[rows, :] = ds

    back = [lax.rem(z + r, LO) for r in range(LO)]

    def give(k, r):
        step = way(k, r)
        return copy(stage.at[k, back[r]], come.at[k, back[r]], up_send.at[k, r], up_recv.at[k, r], at_link(-step))

    def give_wrapped():
        return copy(stage.at[1, z], come.at[1, z], up_send.at[1, 0], up_recv.at[1, 0], at_seq(wrap))

    def gather(k, r):
        return copy(stage.at[k, back[r]], mate.at[k, r], z_send.at[k, r], z_recv.at[k, r], at_lo(r))

    def fill(k, r, *terms):
        total = acc[k, back[r]]
        for t in terms:
            total = total + t.astype(F32)
        stage[k, back[r]] = total.astype(BF16)

    def send(c, k, r, *terms):
        fill(k, r, *terms)
        go(c)

    def came(k, r):
        give(k, r).wait_recv()
        return come[k, back[r]]

    def mates(k):
        for r in (1, 2):
            gather(k, r).wait_recv()
        return mate[k, 1].astype(F32) + mate[k, 2].astype(F32)

    backward(4)
    for r in (1, 2, 0):
        send(give(4, r), 4, r)
    attended = jnp.concatenate([out_t[:, i * HD:(i + 1) * HD].T for i in range(GROUP)], axis=1).astype(BF16)
    att_ref[...] = attended

    def store(i, src, dst):
        c = pltpu.make_async_copy(src, dst, out_sem.at[i])
        c.start()
        return c

    stores = [store(0, att_ref, att_hbm)]

    def part_copy(d):
        m = lax.rem(hi + d, N_HI) * 2 + 1 - core
        return copy(part.at[m], psib.at[d], part_send.at[d], part_recv.at[d], sibling)

    def far_copy(d):
        return copy(pmine.at[d], pfar.at[d], pfar_send.at[d], pfar_recv.at[d], at_hi(d))

    for d in (1, 2, 3, 0):
        m = lax.rem(hi + d, N_HI) * 2 + 1 - core
        part[m] = mm(attended, w[:, pl.ds(pl.multiple_of(m * WIDTH, HD), WIDTH)]).astype(BF16)
        go(part_copy(d))
    backward(5)
    for r in (1, 2):
        send(give(5, r), 5, r)
    for d in (1, 2, 3, 0):
        m = lax.rem(hi + d, N_HI) * 2 + core
        part[m] = mm(attended, w[:, pl.ds(pl.multiple_of(m * WIDTH, HD), WIDTH)]).astype(BF16)
    for d in (1, 2, 3, 0):
        part_copy(d).wait_recv()
        m = lax.rem(hi + d, N_HI) * 2 + core
        both = part[m].astype(F32) + psib[d].astype(F32)
        pmine[d] = both.astype(BF16)
        if d:
            go(far_copy(d))

    scale_rows(0, inv * fade)
    backward(3)
    backward(6)

    for r in (1, 2):
        send(give(3, r), 3, r, came(4, r))
        send(give(6, r), 6, r, came(5, r))
    send(give(3, 0), 3, 0)
    send(give(5, 0), 5, 0, came(4, 0))
    backward(7)
    backward(2)

    for r in (1, 2):
        send(give(2, r), 2, r, came(3, r))
        send(give(7, r), 7, r, came(6, r))
    send(give(2, 0), 2, 0, came(3, 0))
    send(give(6, 0), 6, 0, came(5, 0))
    backward(RING)
    backward(1)
    for r in (1, 2):
        send(give(1, r), 1, r, came(2, r))
        fill(RING, r, came(7, r))
        go_if(not_first, give(RING, r))
        go_if(first, gather(RING, r))
    send(give(7, 0), 7, 0, came(6, 0))
    fill(1, 0, came(2, 0))
    go_if(not_first, give(1, 0))
    go_if(first, give_wrapped())

    @pl.when(first)
    def _():
        fill(RING, 0, came(7, 0), mates(RING))

    @pl.when(last)
    def _():
        fill(RING, 0, came(7, 0), came(1, 0))

    @pl.when(not_first & not_last)
    def _():
        fill(RING, 0, came(7, 0))

    go(give(RING, 0))
    backward(0)
    for r in (1, 2):

        @pl.when(first)
        def _():
            fill(0, r, came(1, r))

        @pl.when(not_first)
        def _():
            fill(0, r, came(1, r), came(RING, r))

        go(gather(0, r))

    dq_t = mm(kt[:, near_part], p_buf[near_part, :]) * fade + mm(kt[:, far_part], p_buf[far_part, :])
    dq_t = dq_t * (inv * SCALE)
    dq_ref[...] = jnp.concatenate([dq_t[:, i * HD:(i + 1) * HD].T for i in range(GROUP)], axis=1).astype(BF16)
    stores.append(store(1, dq_ref, dq_hbm))

    for d in (1, 2, 3):
        far_copy(d).wait_recv()
    mixed_ref[...] = (
        pmine[0].astype(F32) + pfar[1].astype(F32) + pfar[2].astype(F32) + pfar[3].astype(F32)
    ).astype(BF16)
    stores.append(store(2, mixed_ref, mixed_hbm))

    @pl.when(not_last)
    def _():
        acc[0, z] = acc[0, z] + came(1, 0).astype(F32)

    own = acc[0, z]
    own = own + came(RING, 0).astype(F32)
    own = own + mates(0)
    dk_ref[...] = own[0].astype(BF16)
    dv_ref[...] = own[1].astype(BF16)
    stores.append(store(3, dk_ref, dk_hbm))
    stores.append(store(4, dv_ref, dv_hbm))

    for d in (1, 2, 3):
        sent.append((hi + d < N_HI, og_copy(d)))
    for cond, c in sent:
        c.wait_send() if cond is None else pl.when(cond)(c.wait_send)
    for c in stores:
        c.wait()


def finish(*refs):
    for source, target in zip(refs[:5], refs[5:]):
        target[...] = source[...]


def shards(query_heads, key_heads, value_heads, out_weight, out_grad, clip_lengths):
    dma = pltpu.SemaphoreType.DMA
    vmem = pltpu.VMEM
    keys = (RING + 1) * BUNDLE
    hbm = pl.BlockSpec(memory_space=pl.ANY)
    block = jax.ShapeDtypeStruct((TOK, WIDTH), BF16)
    small = jax.ShapeDtypeStruct((TOK, HD), BF16)
    shapes = (block, block, block, small, small)
    piece = (2, TOK, HD)
    results = pl.pallas_call(
        kernel,
        out_shape=shapes,
        in_specs=[pl.BlockSpec(memory_space=pltpu.SMEM)] + [hbm] * 5,
        out_specs=[hbm] * 5,
        scratch_shapes=[
            vmem((TOK, WIDTH), BF16),
            vmem((RING + 1, LO) + piece, BF16),
            vmem((N_HEAD, TOK, WIDTH), BF16),
            vmem((WIDTH, N_HEAD * WIDTH), BF16),
            vmem((HD, WIDTH), BF16),
            vmem((2, WIDTH, HD), BF16),
            vmem((HD, WIDTH), BF16),
            vmem((2, WIDTH, HD), BF16),
            vmem((RING + 1, BUNDLE, WIDTH), F32),
            vmem((keys, WIDTH), BF16),
            vmem((HD, keys), BF16),
            vmem((HD, keys), BF16),
            vmem((8, WIDTH), F32),
            vmem((RING + 1, LO) + piece, F32),
            vmem((N_HEAD, TOK, WIDTH), BF16),
            vmem((N_HI, TOK, WIDTH), BF16),
            vmem((N_HI, TOK, WIDTH), BF16),
            vmem((N_HI, TOK, WIDTH), BF16),
            vmem((RING + 1, LO) + piece, BF16),
            vmem((RING + 1, LO) + piece, BF16),
            vmem((RING + 1, LO) + piece, BF16),
            vmem((TOK, WIDTH), BF16), vmem((TOK, WIDTH), BF16), vmem((TOK, WIDTH), BF16),
            vmem((TOK, HD), BF16), vmem((TOK, HD), BF16),
            dma((5,)), dma((5,)), pltpu.SemaphoreType.REGULAR((N_HI,)),
            dma((RING + 1, LO)), dma((RING + 1, LO)), dma((RING + 1, LO)), dma((RING + 1, LO)),
            dma((N_HI,)), dma((N_HI,)), dma((N_HI,)), dma((N_HI,)),
            dma((N_HI,)), dma((N_HI,)), dma((N_HI,)), dma((N_HI,)),
            dma((RING + 1, LO)), dma((RING + 1, LO)), dma((RING + 1, LO)), dma((RING + 1, LO)),
        ],
        compiler_params=pltpu.CompilerParams(
            collective_id=0, has_side_effects=True, vmem_limit_bytes=60 * 1024 * 1024
        ),
        cost_estimate=pl.CostEstimate(flops=3_000_000_000, bytes_accessed=4_000_000, transcendentals=1_400_000),
    )(clip_lengths, query_heads, key_heads, value_heads, out_grad, out_weight)
    return pl.pallas_call(
        finish,
        out_shape=shapes,
        in_specs=[pl.BlockSpec(memory_space=pltpu.VMEM)] * 5,
        out_specs=[pl.BlockSpec(memory_space=pltpu.VMEM)] * 5,
        compiler_params=pltpu.CompilerParams(vmem_limit_bytes=60 * 1024 * 1024),
    )(*results)


def solution(mesh):
    wide = P("seq", "head")
    return jax.shard_map(
        shards,
        mesh=mesh,
        in_specs=(wide, wide, wide, P("head", None), wide, P()),
        out_specs=(wide,) * 5,
        check_vma=False,
    )
```
